32 devices in a mesh: dp: 4 (over z), expert: 8 (over y, x, core).
Axes of the slice: x: 2, y: 2, z: 4, core: 2. Of those that a mesh axis runs over, the one named last changes fastest.
Arguments:
- tokens: bfloat16 [4096, 2048], P(('dp', 'expert')), may hold values from -6 to 6
- attn_query: bfloat16 [2048, 2048], P(('dp', 'expert')), may hold values from -0.125 to 0.125
- attn_key: bfloat16 [2048, 2048], P(('dp', 'expert')), may hold values from -0.125 to 0.125
- attn_value: bfloat16 [2048, 2048], P(('dp', 'expert')), may hold values from -0.125 to 0.125
- attn_output: bfloat16 [2048, 2048], P(('dp', 'expert')), may hold values from -2 to 2
- norm_in: bfloat16 [2048], P(('dp', 'expert')), may hold values from 0.25 to 1.75
- norm_query: bfloat16 [2048], P(('dp', 'expert')), may hold values from 0.25 to 1.75
- norm_key: bfloat16 [2048], P(('dp', 'expert')), may hold values from 0.25 to 1.75
- norm_mid: bfloat16 [2048], P(('dp', 'expert')), may hold values from 0.25 to 1.75
- router: bfloat16 [2048, 16], P(('dp', 'expert')), may hold values from -0.0625 to 0.0625
- expert_gate: bfloat16 [16, 2048, 1024], P('expert'), may hold values from -0.125 to 0.125
- expert_up: bfloat16 [16, 2048, 1024], P('expert'), may hold values from -0.125 to 0.125
- expert_down: bfloat16 [16, 1024, 2048], P('expert'), may hold values from -0.75 to 0.75
- routes: int32 [4096, 8], P(('dp', 'expert')), may hold values from 0 to 15, all different within a row; in each aligned block of 128 rows (0 to 127, 128 to 255, ...) at most 68 rows name the same one
- pieces: int32 [4096], P(('dp', 'expert')), may hold values from 0 to 5, as said below
- cotangent: bfloat16 [4096, 2048], P(('dp', 'expert')), may hold values from -6 to 6
Outputs:
- output: bfloat16 [4096, 2048], P(('dp', 'expert'))
- input_grad: float32 [4096, 2048], P(('dp', 'expert'))
- query_grad: float32 [2048, 2048], P(('dp', 'expert'))
- key_grad: float32 [2048, 2048], P(('dp', 'expert'))
- value_grad: float32 [2048, 2048], P(('dp', 'expert'))
- output_grad: float32 [2048, 2048], P(('dp', 'expert'))
- norm_in_grad: float32 [2048], P(('dp', 'expert'))
- norm_query_grad: float32 [2048], P(('dp', 'expert'))
- norm_key_grad: float32 [2048], P(('dp', 'expert'))
- norm_mid_grad: float32 [2048], P(('dp', 'expert'))
- router_grad: float32 [2048, 16], P(('dp', 'expert'))
- gate_grad: float32 [16, 2048, 1024], P('expert', 'dp')
- up_grad: float32 [16, 2048, 1024], P('expert', 'dp')
- down_grad: float32 [16, 1024, 2048], P('expert', None, 'dp')
The draws below stay inside these ranges and needn't reach their ends.
Inputs may be any that keep to these rules, and one draw needn't show every extreme that they name: `routes`: each row names 8 different experts. No expert is named by more than 68 of the rows of one device, and in every draw some expert is named by exactly 68 rows of some device. 0 marks text. Tokens of one sequence with the same positive number form one picture piece: consecutive tokens, at most 256 of them, beginning at the sequence's start or at a position p where p + 128 is a multiple of 256. Different pieces of a sequence have different numbers. The last token of every sequence belongs to a picture piece.
All inputs are finite; a program needn't handle non-finite values.
Results may differ from the reference program's by a relative error of at most 0.018.
Values may be sent and summed in bfloat16 or wider, within the bound.
No kernel may reach another device: no remote copies, remote signals or barrier semaphores. Data moves between devices by JAX's collectives and lax.ppermute only.
A program may use at most 320 MiB of HBM per device.

```python
import math
import jax
import jax.numpy as jnp
import numpy as np
from jax import lax

D = 2048
HEADS = 16
HEAD = 128
FF = 1024
TOP = 8
TOK_DEV = 128
PIECE = 256
EXPERTS = 16
LENGTH = 1024
TOKENS = 4096
CAP = 68


def draw_pieces(key, part):
    key = jax.random.fold_in(key, 7)
    block_total = LENGTH // PIECE + 1
    flags = jax.random.randint(key, (TOKENS // LENGTH, block_total), 0, 2)
    position = jnp.arange(LENGTH, dtype=jnp.int32)
    block_index = (position + PIECE // 2) // PIECE
    last_block = (block_index == block_index[LENGTH - 1])[None, :]
    picked = (flags[:, block_index] == 1) | last_block
    numbers = jnp.where(picked, block_index[None, :] + 1, 0)
    return numbers.reshape(TOKENS).astype(jnp.int32)


def steps_of(own_key, dims, shards, low, high):
    level = 1.0
    for dim, shards_of in shards:
        steps = jax.random.uniform(jax.random.fold_in(jax.random.fold_in(own_key, 6), dim), (shards_of,), jnp.float32, low / len(shards), high / len(shards))
        level = level * jnp.repeat(jnp.exp(steps), dims[dim] // shards_of).reshape((-1,) + (1,) * (len(dims) - 1 - dim))
    return level


def deal_out(rng, own, number, rows, number_of, top, reach, slope):
    sequence = jax.random.permutation(rng, number_of)
    heavy_load, common = portions_of(number_of, rows * top, reach, slope, True), portions_of(number_of, rows * top, reach, slope, False)
    places = jnp.arange(number_of)

    def named(lengths, turn):
        used = int((lengths > 0).sum())
        fixed = max(1, used // 4)
        shifted = fixed + (places - fixed + turn * (used - fixed)) % max(1, number_of - fixed)
        return jnp.zeros((number_of,), jnp.int32).at[sequence[jnp.where(places < fixed, places, shifted)]].set(jnp.asarray(lengths, jnp.int32))

    lengths = jnp.where(number % 4 == 0, named(heavy_load, number // 4), named(common, number - number // 4 - 1))
    mixed = jax.random.permutation(jax.random.fold_in(own, 3), number_of)
    source_of, taker = mixed[0:number_of // 2 * 2:2], mixed[1:number_of // 2 * 2:2]
    slack = jnp.minimum(lengths[source_of] - 1, reach - lengths[taker]) // 2
    slack = jnp.where((source_of == sequence[0]) | (taker == sequence[0]) | (lengths[taker] == 0), 0, jnp.maximum(slack, 0))
    shifted = jax.random.randint(jax.random.fold_in(own, 4), (number_of // 2,), 0, 1 << 20) % (slack + 1)
    lengths = lengths.at[source_of].add(-shifted).at[taker].add(shifted)
    labels = jnp.searchsorted(jnp.cumsum(lengths), jnp.arange(rows * top), side="right").astype(jnp.int32)
    table = labels.reshape(top, rows).T
    table = table[jax.random.permutation(jax.random.fold_in(own, 1), rows)]
    turn = jax.random.randint(jax.random.fold_in(own, 2), (rows, 1), 0, top)
    return jnp.take_along_axis(table, (jnp.arange(top)[None, :] + turn) % top, axis=1)


def portions_of(number_of, total, bound, lean, full):
    portions = [(1 << 20) // math.isqrt(rank ** lean) + 1 for rank in range(1, number_of + 1)]
    largest = bound if full else min(bound, max(-(-total // number_of), total * portions[0] // sum(portions)))
    least = 1 if total - largest >= number_of - 1 else 0
    holding, rest = [largest] + [least] * (number_of - 1), total - largest - least * (number_of - 1)
    while rest > 0:
        movable = [i for i in range(1, number_of) if holding[i] < largest] or [i for i in range(1, number_of) if holding[i] < bound]
        whole, left = sum([portions[i] for i in movable]), rest
        for i in movable:
            addition = min(bound - holding[i], max(1, left * portions[i] // whole), rest)
            holding[i] = holding[i] + addition
            rest = rest - addition
    return np.array(holding)


def gaussian(own_key, dims, spread, bound, split=(), held_as=jnp.bfloat16):
    array = jax.random.normal(own_key, dims, jnp.float32) * spread
    if len(split) > 0:
        array = steps_of(own_key, dims, split, -0.22, 0.18) * array
    return jnp.clip(array, min=-bound, max=bound).astype(held_as)


def setup_inputs(seed: int = 0) -> dict:
    splits = jax.random.split(jax.random.key(seed), 17)
    tokens = gaussian(splits[0], (TOKENS, D), 1.0, 6.0, ((0, 32),))
    attn_query = gaussian(splits[1], (D, D), D ** -0.5, 0.125, ((0, 32),))
    attn_key = gaussian(splits[2], (D, D), D ** -0.5, 0.125, ((0, 32),))
    attn_value = gaussian(splits[3], (D, D), D ** -0.5, 0.125, ((0, 32),))
    attn_output = gaussian(splits[4], (D, D), (max(D // 256, 1)) ** -0.5, 2.0, ((0, 32),))
    norm_in = jnp.clip(1.0 + 0.15 * jax.random.normal(splits[5], (D,), jnp.float32), 0.25, 1.75).astype(jnp.bfloat16)
    norm_query = jnp.clip(1.0 + 0.15 * jax.random.normal(splits[6], (D,), jnp.float32), 0.25, 1.75).astype(jnp.bfloat16)
    norm_key = jnp.clip(1.0 + 0.15 * jax.random.normal(splits[7], (D,), jnp.float32), 0.25, 1.75).astype(jnp.bfloat16)
    norm_mid = jnp.clip(1.0 + 0.15 * jax.random.normal(splits[8], (D,), jnp.float32), 0.25, 1.75).astype(jnp.bfloat16)
    router = gaussian(splits[9], (D, EXPERTS), (4 * D) ** -0.5, 0.0625, ((0, 32),))
    expert_gate = gaussian(splits[10], (EXPERTS, D, FF), D ** -0.5, 0.125, ((0, 8),))
    expert_up = gaussian(splits[11], (EXPERTS, D, FF), D ** -0.5, 0.125, ((0, 8),))
    expert_down = gaussian(splits[12], (EXPERTS, FF, D), (max(FF // 16, 1)) ** -0.5, 0.75, ((0, 8),))
    routes_keys = jax.random.split(jax.random.fold_in(splits[13], 1), TOKENS // TOK_DEV)
    routes_turns = jax.random.permutation(jax.random.fold_in(splits[13], 3), TOKENS // TOK_DEV)
    routes = jax.vmap(lambda own, number: deal_out(jax.random.fold_in(splits[13], 2), own, number, TOK_DEV, EXPERTS, TOP, CAP, 1))(routes_keys, routes_turns).reshape((TOKENS, TOP))
    pieces = draw_pieces(jax.random.fold_in(splits[16], 71), 0)
    cotangent = gaussian(splits[15], (TOKENS, D), 1.0, 6.0, ((0, 32),))
    return dict(tokens=tokens, attn_query=attn_query, attn_key=attn_key, attn_value=attn_value, attn_output=attn_output, norm_in=norm_in, norm_query=norm_query, norm_key=norm_key, norm_mid=norm_mid, router=router, expert_gate=expert_gate, expert_up=expert_up, expert_down=expert_down, routes=routes, pieces=pieces, cotangent=cotangent)


@jax.custom_vjp
def low(v):
    return lax.optimization_barrier(v.astype(jnp.bfloat16)).astype(jnp.float32)

@jax.custom_vjp
def low_back(v):
    return v

def low_keep(v):
    return (low(v), None)

def low_pass(kept, grad):
    return (grad,)

def back_keep(v):
    return (v, None)

def back_low(kept, grad):
    return (low(grad),)
low.defvjp(low_keep, low_pass)
low_back.defvjp(back_keep, back_low)
eps_norm = 1e-05
rope_base = 10000.0

def product(left, right):
    return jnp.dot(left, right, preferred_element_type=jnp.float32, precision=lax.Precision.HIGHEST)

def rms_scale(values, gain_vector):
    return values * lax.rsqrt(lax.optimization_barrier(jnp.mean(values * values, axis=-1, keepdims=True)) + eps_norm) * gain_vector

def angle_tables(positions, head_size):
    half_size = head_size // 2
    inverse = jnp.exp(jnp.arange(half_size, dtype=jnp.float32) * (-2.0 * math.log(rope_base) / head_size))
    angles = positions[:, None] * inverse[None, :]
    return (jnp.cos(angles)[:, None, :], jnp.sin(angles)[:, None, :])

def rotate(values, cosine, sine_table):
    half_size = values.shape[-1] // 2
    first_half = values[..., :half_size]
    second = values[..., half_size:]
    return jnp.concatenate([first_half * cosine - second * sine_table, second * cosine + first_half * sine_table], axis=-1)

def softmax_rows(scores):
    highest = lax.optimization_barrier(jnp.max(scores, axis=-1, keepdims=True))
    exponent = jnp.exp(scores - highest)
    return exponent / lax.optimization_barrier(jnp.sum(exponent, axis=-1, keepdims=True))

def layer(hidden_in, weights, route_rows, piece_rows):
    attn_query, attn_key, attn_value, attn_output, norm_in, norm_query, norm_key, norm_mid, router, expert_gate, expert_up, expert_down = weights
    length = hidden_in.shape[0]
    normed = low(rms_scale(hidden_in, norm_in))
    query_raw = low_back(product(normed, attn_query))
    key_raw = low_back(product(normed, attn_key))
    value_raw = low_back(product(normed, attn_value))
    cosine, sine_table = angle_tables(jnp.arange(length, dtype=jnp.float32), HEAD)
    queries = low(rotate(rms_scale(query_raw, norm_query).reshape(length, HEADS, HEAD), cosine, sine_table))
    key_rows = low(rotate(rms_scale(key_raw, norm_key).reshape(length, HEADS, HEAD), cosine, sine_table))
    value_rows = low(value_raw).reshape(length, HEADS, HEAD)
    scores = low_back(jnp.einsum('qhd,khd->hqk', queries, key_rows, precision=lax.Precision.HIGHEST) * HEAD ** (-0.5))
    position = jnp.arange(length)
    earlier = position[None, :] <= position[:, None]
    same_piece = (piece_rows[:, None] == piece_rows[None, :]) & (piece_rows[:, None] > 0)
    allowed = earlier | same_piece
    probabilities = low(softmax_rows(jnp.where(allowed[None], scores, -1e+30)))
    mixed_heads = jnp.einsum('hqk,khd->qhd', probabilities, value_rows, precision=lax.Precision.HIGHEST).reshape(length, D)
    attended = low(low_back(mixed_heads))
    residual = hidden_in + low_back(product(attended, attn_output))
    normed_mid = low(rms_scale(residual, norm_mid))
    logits = low_back(product(normed_mid, router))
    router_probs = softmax_rows(logits)
    chosen = lax.optimization_barrier(jnp.sum((route_rows[:, :, None] == jnp.arange(EXPERTS)[None, None, :]).astype(jnp.float32), axis=1))
    gate_weights = router_probs * chosen

    def expert_term(running, packed):
        weight_gate, weight_up, weight_down, gate_column = packed
        entered = low_back(normed_mid)
        gate_act = low_back(product(entered, weight_gate))
        up_act = low_back(product(entered, weight_up))
        hidden = low(jax.nn.silu(gate_act) * up_act)
        returned = low(low_back(product(hidden, weight_down)))
        return (running + gate_column[:, None] * returned, None)
    moe_out, unused = lax.scan(jax.checkpoint(expert_term), jnp.zeros_like(residual), (expert_gate, expert_up, expert_down, gate_weights.T))
    return residual + moe_out

def reference(tokens, attn_query, attn_key, attn_value, attn_output, norm_in, norm_query, norm_key, norm_mid, router, expert_gate, expert_up, expert_down, routes, pieces, cotangent):
    weights = tuple((weight.astype(jnp.float32) for weight in (attn_query, attn_key, attn_value, attn_output, norm_in, norm_query, norm_key, norm_mid, router, expert_gate, expert_up, expert_down)))
    sequences = TOKENS // LENGTH
    token_seqs = tokens.astype(jnp.float32).reshape(sequences, LENGTH, D)
    cot_seqs = cotangent.astype(jnp.float32).reshape(sequences, LENGTH, D)
    route_seqs = routes.reshape(sequences, LENGTH, TOP)
    piece_seqs = pieces.reshape(sequences, LENGTH)

    def one_sequence(totals, packed):
        hidden_in, cot_in, route_in, piece_in = packed

        def forward(values, params):
            return layer(values, params, route_in, piece_in)
        result, pullback = jax.vjp(forward, hidden_in, weights)
        grad_in, grad_weights = pullback(cot_in)
        totals = tuple((running + gradient for running, gradient in zip(totals, grad_weights)))
        return (totals, (result.astype(jnp.bfloat16), grad_in))
    initial = tuple((jnp.zeros(weight.shape, jnp.float32) for weight in weights))
    totals, (outputs, grads_in) = lax.scan(one_sequence, initial, (token_seqs, cot_seqs, route_seqs, piece_seqs))
    query_grad, key_grad, value_grad, output_grad, norm_in_grad, norm_query_grad, norm_key_grad, norm_mid_grad, router_grad, gate_grad, up_grad, down_grad = totals
    return (outputs.reshape(TOKENS, D), grads_in.reshape(TOKENS, D), query_grad, key_grad, value_grad, output_grad, norm_in_grad, norm_query_grad, norm_key_grad, norm_mid_grad, router_grad, gate_grad, up_grad, down_grad)
```

```python
import math

import jax
import jax.numpy as jnp
from jax import lax
from jax.sharding import PartitionSpec as P

HEAD = 128
eps_norm = 1e-05
rope_base = 10000.0
single = jnp.float32
bfloat = jnp.bfloat16


def dot32(left, right, dims):
    return lax.dot_general(left, right, (dims, ((), ())), preferred_element_type=single)


def swap(values, axis, mask):
    count = lax.axis_size(axis)
    return lax.ppermute(values, axis, [(i, i ^ mask) for i in range(count)])


def gather_each(values, axis):
    count = lax.axis_size(axis)
    return [values] + [swap(values, axis, mask) for mask in range(1, count)]


def gather_pairs(values):
    count = lax.axis_size("expert")
    blocks = [None] * count
    for mask in range(0, count, 2):
        blocks[mask] = values if mask == 0 else swap(values, "expert", mask)
        blocks[mask + 1] = swap(blocks[mask], "expert", 1)
    return blocks


def gather_steps(values, axis, count):
    held = values[None]
    order = [0]
    mask = count - 1
    while mask > 0:
        other = swap(held, axis, mask)
        held = jnp.concatenate([held, other], axis=0)
        order = order + [place ^ mask for place in order]
        mask >>= 1
    return held, order


def scatter_sum_pairs(parts):
    count = len(parts)
    odd = jnp.stack([parts[mask + 1] for mask in range(0, count, 2)])
    arrived = swap(odd, "expert", 1)
    sums = [
        (parts[mask].astype(single) + arrived[mask // 2].astype(single)).astype(bfloat)
        for mask in range(0, count, 2)
    ]
    total = sums[0].astype(single)
    for place in range(1, count // 2):
        total = total + swap(sums[place], "expert", 2 * place).astype(single)
    return total


def sum_rows_over_expert(values):
    count = lax.axis_size("expert")

    def reorder(array, mask):
        return jnp.concatenate(
            [array[..., j ^ mask : (j ^ mask) + 1, :] for j in range(count)], axis=-2
        )

    total = values + reorder(swap(values, "expert", 1), 1)
    out = total
    for mask in range(2, count, 2):
        out = out + reorder(swap(total, "expert", mask), mask)
    return out


def permute_blocks(array, mask, count):
    rows = array.shape[0] // count
    if mask == 0:
        return array
    return jnp.concatenate(
        [array[(j ^ mask) * rows : ((j ^ mask) + 1) * rows] for j in range(count)], axis=0
    )


def per_device(
    tokens,
    attn_query,
    attn_key,
    attn_value,
    attn_output,
    norm_in,
    norm_query,
    norm_key,
    norm_mid,
    router,
    expert_gate,
    expert_up,
    expert_down,
    routes,
    pieces,
    cotangent,
):
    n = lax.axis_size("expert")
    m = lax.axis_size("dp")
    rows, model = tokens.shape
    shard = attn_query.shape[0]
    experts = router.shape[1]
    local = expert_gate.shape[0]
    hidden_units = expert_gate.shape[2]
    length = rows * n
    near = min(m, 4)
    width = model // n
    heads = width // HEAD
    mine = lax.axis_index("expert")
    plane = lax.axis_index("dp")
    scale = HEAD ** (-0.5)
    slots = jnp.arange(n, dtype=jnp.int32) ^ mine

    small = jnp.concatenate(
        [norm_in[None], norm_query[None], norm_key[None], norm_mid[None], router.T], axis=0
    )
    kinds = small.shape[0]
    small = jnp.stack(gather_each(small, "dp"))
    small = jnp.stack(gather_each(small, "expert"))
    small = jnp.take(small, slots, axis=0)
    small = jnp.take(small, jnp.arange(m, dtype=jnp.int32) ^ plane, axis=1)
    small = small.transpose(2, 1, 0, 3).reshape(kinds, model)
    gain_in, gain_query, gain_key, gain_mid = [small[i].astype(single) for i in range(4)]
    router_t = small[4:]

    info = jnp.concatenate([routes.T, pieces[None]], axis=0)
    info = jnp.stack(gather_each(info, "expert"), axis=1)
    info = jnp.stack(gather_each(info, "dp"))
    piece_row = info[0, -1].reshape(length)

    x_b = jnp.concatenate(gather_pairs(tokens), axis=0)
    packed = jnp.stack([attn_query, attn_key, attn_value]).reshape(3, shard, n, width)
    packed = packed.transpose(2, 0, 1, 3)
    packed = lax.all_to_all(packed, "expert", split_axis=0, concat_axis=0, tiled=True)
    packed = packed.transpose(1, 0, 2, 3).reshape(3, n * shard, width)
    w_qk = lax.all_gather(packed[:2], "dp", axis=1, tiled=True)
    w_v = lax.all_gather(packed[2], "dp", axis=0, tiled=True)
    w_q, w_k = w_qk[0], w_qk[1]
    wo_full = lax.all_gather(attn_output, ("dp", "expert"), axis=0, tiled=True)
    wo = jnp.take(wo_full.reshape(n, width, model), slots, axis=0).reshape(model, model)
    wo_own = lax.dynamic_slice_in_dim(wo_full, mine * width, width, 0)

    x = x_b.astype(single)
    rs_in = lax.rsqrt(jnp.mean(x * x, axis=-1, keepdims=True) + eps_norm)
    normed_b = (x * rs_in * gain_in).astype(bfloat)
    query_raw = dot32(normed_b, w_q, ((1,), (0,)))
    key_raw = dot32(normed_b, w_k, ((1,), (0,)))
    squares = jnp.stack([jnp.sum(query_raw**2, axis=-1), jnp.sum(key_raw**2, axis=-1)])
    squares = sum_rows_over_expert(squares.reshape(2, n, rows)).reshape(2, length)
    rs_q = lax.rsqrt(squares[0] / model + eps_norm)[:, None]
    rs_k = lax.rsqrt(squares[1] / model + eps_norm)[:, None]
    value_b = dot32(normed_b, w_v, ((1,), (0,))).astype(bfloat)

    place = (slots[:, None] * rows + jnp.arange(rows, dtype=jnp.int32)[None, :]).reshape(length)
    half = HEAD // 2
    inverse = jnp.exp(jnp.arange(half, dtype=single) * (-2.0 * math.log(rope_base) / HEAD))
    angles = place.astype(single)[:, None] * inverse[None, :]
    cosine = jnp.cos(angles)
    sine = jnp.sin(angles)

    def rotate(values, back):
        out = []
        sn = -sine if back else sine
        for h in range(heads):
            u = values[:, h * HEAD : h * HEAD + half]
            w = values[:, h * HEAD + half : (h + 1) * HEAD]
            out += [u * cosine - w * sn, w * cosine + u * sn]
        return jnp.concatenate(out, axis=-1)

    own_gain_q = lax.dynamic_slice_in_dim(gain_query, mine * width, width)
    own_gain_k = lax.dynamic_slice_in_dim(gain_key, mine * width, width)
    query_b = rotate(query_raw * rs_q * own_gain_q, False).astype(bfloat)
    key_b = rotate(key_raw * rs_k * own_gain_k, False).astype(bfloat)

    def per_head(array):
        return [array[:, h * HEAD : (h + 1) * HEAD] for h in range(heads)]

    allowed = (place[None, :] <= place[:, None]) | (
        (piece_row[:, None] == piece_row[None, :]) & (piece_row[:, None] > 0)
    )
    probs = []
    mixed = []
    for q_h, k_h, v_h in zip(per_head(query_b), per_head(key_b), per_head(value_b)):
        scores = jnp.where(allowed, dot32(q_h, k_h, ((1,), (1,))) * scale, -1e30)
        exponent = jnp.exp(scores - jnp.max(scores, axis=-1, keepdims=True))
        prob = exponent / jnp.sum(exponent, axis=-1, keepdims=True)
        probs.append(prob)
        mixed.append(dot32(prob.astype(bfloat), v_h, ((1,), (0,))))
    attended = jnp.concatenate(mixed, axis=-1).astype(bfloat)
    att = gather_pairs(attended)
    att = jnp.concatenate([permute_blocks(att[k], k, n) for k in range(n)], axis=1)

    residual = x + dot32(att, wo, ((1,), (0,)))
    rs_mid = lax.rsqrt(jnp.mean(residual * residual, axis=-1, keepdims=True) + eps_norm)
    mid = (residual * rs_mid * gain_mid).astype(bfloat)

    def other_planes(own_block):
        held, order = gather_steps(own_block, "dp", near)
        blocks = gather_pairs(held[1:])
        return jnp.stack(blocks, axis=1)

    cot_plane = jnp.concatenate(gather_pairs(cotangent), axis=0)
    cot_others = other_planes(cotangent)
    mid_others = other_planes(mid[:rows])
    order = gather_steps(jnp.zeros((), jnp.int32), "dp", near)[1]

    def router_probs_of(mid_rows):
        logits = dot32(mid_rows, router_t, ((1,), (1,)))
        exponent = jnp.exp(logits - jnp.max(logits, axis=-1, keepdims=True))
        return exponent / jnp.sum(exponent, axis=-1, keepdims=True)

    block = 2 * rows
    cap = 2 * min(rows, rows * routes.shape[1] // experts + rows // 32)
    upper = (
        jnp.arange(block, dtype=jnp.int32)[:, None] <= jnp.arange(block, dtype=jnp.int32)[None, :]
    ).astype(bfloat)

    def picks(route_rows):
        ids = mine * local + jnp.arange(local, dtype=jnp.int32)
        hit = jnp.any(route_rows[:, None] == ids[None, :, None, None], axis=2)
        rank = lax.dot_general(
            hit.astype(bfloat), upper, (((2,), (0,)), ((), ())), preferred_element_type=single
        )
        wanted = jnp.arange(1, cap + 1, dtype=jnp.int32).astype(single)
        return hit[:, :, None, :] & (rank[:, :, None, :] == wanted[None, None, :, None])

    def expert_rows(mid_rows, cot_rows, route_rows):
        groups = route_rows.shape[0]
        router_probs = router_probs_of(mid_rows)
        local_probs = lax.dynamic_slice_in_dim(router_probs, mine * local, local, 1)
        local_probs = local_probs.reshape(groups, block, local).transpose(0, 2, 1)
        pick = picks(route_rows)
        pick_b = pick.astype(bfloat)
        gate_row = jnp.sum(jnp.where(pick, local_probs[:, :, None, :], 0.0), axis=-1)
        entered = jnp.einsum("gjct,gtd->jgcd", pick_b, mid_rows.reshape(groups, block, model))
        cot_row = jnp.einsum("gjct,gtd->jgcd", pick_b, cot_rows.reshape(groups, block, model))
        dreturned = (gate_row.transpose(1, 0, 2)[..., None] * cot_row.astype(single)).astype(bfloat)
        gate_act = jnp.einsum("jgcd,jdf->jgcf", entered, expert_gate, preferred_element_type=single)
        up_act = jnp.einsum("jgcd,jdf->jgcf", entered, expert_up, preferred_element_type=single)
        sig = jax.nn.sigmoid(gate_act)
        silu = gate_act * sig
        hidden = (silu * up_act).astype(bfloat)
        dhidden = jnp.einsum(
            "jgcd,jfd->jgcf", dreturned, expert_down, preferred_element_type=single
        )
        gate_lin = (dhidden * up_act * sig * (1.0 + gate_act * (1.0 - sig))).astype(bfloat)
        up_lin = (dhidden * silu).astype(bfloat)
        return router_probs, local_probs, pick, pick_b, entered, cot_row, dreturned, hidden, gate_lin, up_lin

    def groups_of(info_planes):
        planes = info_planes.shape[0]
        r = info_planes[:, :-1].reshape(planes, -1, n // 2, block)
        return r.transpose(0, 2, 1, 3).reshape(planes * n // 2, -1, block)

    own_groups = groups_of(info[:1])
    (router_probs, local_probs, pick, pick_b, entered, cot_row, dreturned, hidden, gate_lin, up_lin) = (
        expert_rows(mid, cot_plane, own_groups)
    )
    returned = jnp.einsum(
        "jgcf,jfd->jgcd", hidden, expert_down, preferred_element_type=single
    ).astype(bfloat)
    dgate_row = jnp.sum(cot_row.astype(single) * returned.astype(single), axis=-1)
    dmid_rows = (
        jnp.einsum("jgcf,jdf->jgcd", gate_lin, expert_gate, preferred_element_type=single)
        + jnp.einsum("jgcf,jdf->jgcd", up_lin, expert_up, preferred_element_type=single)
    ).astype(bfloat)
    dmid = jnp.einsum(
        "gjct,jgcd->gtd", pick_b, dmid_rows, preferred_element_type=single
    ).reshape(length, model)
    dprobs = jnp.sum(
        jnp.where(pick, dgate_row.transpose(1, 0, 2)[..., None], 0.0), axis=2
    )
    dprobs = dprobs.transpose(0, 2, 1).reshape(length, local)
    dprobs = lax.dynamic_update_slice(
        jnp.zeros((length, experts), single), dprobs, (jnp.zeros((), jnp.int32), mine * local)
    )
    dlogits = router_probs * (dprobs - jnp.sum(router_probs * dprobs, axis=-1, keepdims=True))
    dlogits_b = dlogits.astype(bfloat)
    router_grad = dot32(dlogits_b, mid, ((0,), (0,)))
    dmid = dmid + dot32(dlogits_b, router_t, ((1,), (0,)))
    mid_grad = jnp.sum(dmid * (residual * rs_mid), axis=0)
    scaled = dmid * gain_mid
    inner = jnp.mean(scaled * residual, axis=-1, keepdims=True)
    dres_part = (rs_mid * (scaled - residual * (rs_mid * rs_mid * inner))).astype(bfloat)

    datt_all = dot32(dres_part, wo, ((1,), (1,))).astype(bfloat)
    datt = scatter_sum_pairs(
        [permute_blocks(datt_all[:, k * width : (k + 1) * width], k, n) for k in range(n)]
    )
    datt = datt + dot32(cot_plane, wo_own, ((1,), (1,)))
    datt_b = datt.astype(bfloat)
    dq_rot, dk_rot, dv = [], [], []
    for prob, da, q_h, k_h, v_h in zip(
        probs, per_head(datt_b), per_head(query_b), per_head(key_b), per_head(value_b)
    ):
        dprob = dot32(da, v_h, ((1,), (1,)))
        dsum = jnp.sum(prob * dprob, axis=-1, keepdims=True)
        dscores = (prob * (dprob - dsum)).astype(bfloat)
        dv.append(dot32(prob.astype(bfloat), da, ((0,), (0,))))
        dq_rot.append(dot32(dscores, k_h, ((1,), (0,))) * scale)
        dk_rot.append(dot32(dscores, q_h, ((0,), (0,))) * scale)
    dq_un = rotate(jnp.concatenate(dq_rot, axis=-1), True)
    dk_un = rotate(jnp.concatenate(dk_rot, axis=-1), True)
    inners = jnp.stack(
        [
            jnp.sum(dq_un * own_gain_q * query_raw, axis=-1),
            jnp.sum(dk_un * own_gain_k * key_raw, axis=-1),
        ]
    )
    inners = sum_rows_over_expert(inners.reshape(2, n, rows)).reshape(2, length)
    query_gain_grad = jnp.sum(dq_un * query_raw * rs_q, axis=0)
    key_gain_grad = jnp.sum(dk_un * key_raw * rs_k, axis=0)
    dq_b = (
        rs_q * dq_un * own_gain_q - query_raw * (rs_q**3 / model * inners[0][:, None])
    ).astype(bfloat)
    dk_b = (
        rs_k * dk_un * own_gain_k - key_raw * (rs_k**3 / model * inners[1][:, None])
    ).astype(bfloat)
    dv_b = jnp.concatenate(dv, axis=-1).astype(bfloat)
    dnormed_part = (
        dot32(dq_b, w_q, ((1,), (1,)))
        + dot32(dk_b, w_k, ((1,), (1,)))
        + dot32(dv_b, w_v, ((1,), (1,)))
    ).astype(bfloat)

    def own_rows(array, k):
        return array[k * rows : (k + 1) * rows]

    dnormed = scatter_sum_pairs([own_rows(dnormed_part, k) for k in range(n)])

    def weight_sum(partial):
        summed = lax.psum_scatter(
            partial.astype(bfloat), "dp", scatter_dimension=0, tiled=True
        )
        moved = lax.all_to_all(
            summed.reshape(n, shard, width), "expert", split_axis=0, concat_axis=0, tiled=True
        )
        return moved.transpose(1, 0, 2).reshape(shard, model).astype(single)

    value_grad = weight_sum(dot32(normed_b, dv_b, ((0,), (0,))))
    query_grad = weight_sum(dot32(normed_b, dq_b, ((0,), (0,))))
    key_grad = weight_sum(dot32(normed_b, dk_b, ((0,), (0,))))

    moe_part = jnp.einsum(
        "gjct,jgcd->gtd",
        jnp.where(pick, local_probs[:, :, None, :], 0.0).astype(bfloat),
        returned,
        preferred_element_type=single,
    ).astype(bfloat).reshape(length, model)
    moe = scatter_sum_pairs([own_rows(moe_part, k) for k in range(n)])
    output = (residual[:rows] + moe).astype(bfloat)
    dres = scatter_sum_pairs([own_rows(dres_part, k) for k in range(n)])
    dres = dres + cotangent.astype(single)
    dres_b = dres.astype(bfloat)
    cols = dres_b.reshape(rows, n, width).transpose(1, 0, 2)
    cols = jnp.take(cols, slots, axis=0)
    cols = jnp.concatenate(
        [cols[0]] + [swap(cols[k], "expert", k) for k in range(1, n)], axis=0
    )
    output_part = dot32(att, cols, ((0,), (0,)))
    output_part = jnp.take(output_part.reshape(n, width, width), slots, axis=0)
    output_grad = weight_sum(output_part.reshape(model, width))

    other_info = jnp.stack([info[k] for k in order[1:]])
    other = expert_rows(
        mid_others.reshape(-1, model), cot_others.reshape(-1, model), groups_of(other_info)
    )

    def rows_of(own_part, other_part):
        return jnp.concatenate(
            [
                own_part.reshape(local, -1, own_part.shape[-1]),
                other_part.reshape(local, -1, other_part.shape[-1]),
            ],
            axis=1,
        )

    span = model // m
    far = m // near

    def cut(array):
        parts = array.reshape(array.shape[:2] + (far, near, span))
        parts = lax.dynamic_index_in_dim(parts, plane % near, 3, keepdims=False)
        return parts.reshape(array.shape[:2] + (far * span,))

    def sum_over_far(parts):
        if far == 1:
            return parts[0]
        parts = jnp.take(parts, jnp.arange(far, dtype=jnp.int32) ^ (plane // near), axis=0)
        total = parts[0]
        for k in range(1, far):
            total = total + swap(parts[k].astype(bfloat), "dp", k * near).astype(single)
        return total

    hidden_all = rows_of(hidden, other[7])
    gate_all = rows_of(gate_lin, other[8])
    up_all = rows_of(up_lin, other[9])
    entered_cut = cut(rows_of(entered, other[4]))
    dret_cut = cut(rows_of(dreturned, other[6]))
    gate_grad = jnp.einsum("jrd,jrf->jdf", entered_cut, gate_all, preferred_element_type=single)
    up_grad = jnp.einsum("jrd,jrf->jdf", entered_cut, up_all, preferred_element_type=single)
    down_grad = jnp.einsum("jrf,jrd->jfd", hidden_all, dret_cut, preferred_element_type=single)
    gate_grad, up_grad = [
        sum_over_far(
            grad.reshape(local, far, span, hidden_units).transpose(1, 0, 2, 3)
        )
        for grad in (gate_grad, up_grad)
    ]
    down_grad = sum_over_far(
        down_grad.reshape(local, hidden_units, far, span).transpose(2, 0, 1, 3)
    )

    x_own = tokens.astype(single)
    rs_own = rs_in[:rows]
    scaled_in = dnormed * gain_in
    inner_in = jnp.mean(scaled_in * x_own, axis=-1, keepdims=True)
    input_grad = dres + rs_own * (scaled_in - x_own * (rs_own * rs_own * inner_in))
    in_grad = jnp.sum(dnormed * x_own * rs_own, axis=0)

    def placed(part):
        return lax.dynamic_update_slice(jnp.zeros((model,), single), part, (mine * width,))

    small_grad = jnp.concatenate(
        [
            in_grad[None],
            placed(query_gain_grad)[None],
            placed(key_gain_grad)[None],
            mid_grad[None],
            router_grad,
        ],
        axis=0,
    ).reshape(kinds, m, n, shard)
    small_grad = jnp.take(small_grad, slots, axis=2)
    small_sum = small_grad[:, :, 0]
    for k in range(1, n):
        small_sum = small_sum + swap(small_grad[:, :, k], "expert", k)
    small_sum = jnp.take(small_sum, jnp.arange(m, dtype=jnp.int32) ^ plane, axis=1)
    total = small_sum[:, 0]
    for k in range(1, m):
        total = total + swap(small_sum[:, k], "dp", k)

    return (
        output,
        input_grad,
        query_grad,
        key_grad,
        value_grad,
        output_grad,
        total[0],
        total[1],
        total[2],
        total[3],
        total[4:].T,
        gate_grad,
        up_grad,
        down_grad,
    )


def solution(mesh):
    both = ("dp", "expert")
    in_specs = (
        [P(both, None)] * 5
        + [P(both)] * 4
        + [P(both, None)]
        + [P("expert", None, None)] * 3
        + [P(both, None), P(both), P(both, None)]
    )
    out_specs = (
        [P(both, None)] * 6
        + [P(both)] * 4
        + [P(both, None)]
        + [P("expert", "dp", None)] * 2
        + [P("expert", None, "dp")]
    )
    return jax.shard_map(
        per_device,
        mesh=mesh,
        in_specs=tuple(in_specs),
        out_specs=tuple(out_specs),
        check_vma=False,
    )
```

```python
import functools
import math

import jax
import jax.numpy as jnp
from jax import lax
from jax.experimental import pallas as pl
from jax.experimental.pallas import tpu as pltpu
from jax.sharding import PartitionSpec as P

HEAD = 128
eps_norm = 1e-05
rope_base = 10000.0
single = jnp.float32
bfloat = jnp.bfloat16


def dot32(left, right, dims):
    return lax.dot_general(left, right, (dims, ((), ())), preferred_element_type=single)


def after(values, *earlier):
    for result in earlier:
        zero = jnp.minimum(jnp.abs(result[(-1,) * result.ndim]), 0)
        values = values + zero.astype(values.dtype)
    return values


def swap(values, axis, mask):
    count = lax.axis_size(axis)
    return lax.ppermute(values, axis, [(i, i ^ mask) for i in range(count)])


def slot_order():
    count = lax.axis_size("expert")
    return list(range(0, count, 2)) + list(range(1, count, 2))


def gather_chips(values):
    count = lax.axis_size("expert")
    return [values if mask == 0 else swap(values, "expert", mask) for mask in range(0, count, 2)]


def gather_halves(values, *earlier):
    even = after(jnp.stack(gather_chips(values)), *earlier)
    return even, swap(even, "expert", 1)


def gather_steps(values, axis, count, first=None):
    held = values[None]
    order = [0]
    mask = count - 1
    while mask > 0:
        other = first if first is not None and mask == count - 1 else swap(held, axis, mask)
        held = jnp.concatenate([held, other], axis=0)
        order = order + [place ^ mask for place in order]
        mask >>= 1
    return held, order


def scatter_sum(even, odd, with_first=False):
    half = lax.axis_size("expert") // 2
    rows = even.shape[0] // half
    arrived = swap(odd, "expert", 1)
    total = None
    for place in reversed(range(half)):
        part = slice(place * rows, (place + 1) * rows)
        pair = even[part].astype(single) + arrived[part].astype(single)
        if place > 0:
            pair = swap(pair.astype(bfloat), "expert", 2 * place).astype(single)
        if place == half - 1:
            first = arrived
        total = pair if total is None else total + pair
    return (total, first) if with_first else total


def sum_rows_over_expert(values):
    order = slot_order()

    def reorder(array, mask):
        return jnp.concatenate(
            [array[:, order.index(s ^ mask)][:, None] for s in order], axis=1
        )

    total = values + reorder(swap(values, "expert", 1), 1)
    out = total
    for mask in range(2, len(order), 2):
        out = out + reorder(swap(total, "expert", mask), mask)
    return out


def rows_of_group(pieces, g, groups, ids_ref):
    if len(pieces) == 2:
        return jnp.concatenate([pieces[0][0, g], pieces[1][0, g]], axis=0)
    if len(pieces) > 2:
        return jnp.concatenate([pieces[g][0], pieces[groups + g][0]], axis=0)
    at = 2 + ids_ref[1]
    return jnp.concatenate(
        [pieces[0][0, ids_ref[at + 2 * g]], pieces[0][0, ids_ref[at + 2 * g + 1]]], axis=0
    )


def enter_rows(ids_ref, rank_ref, prob_ref, mid_refs, cot_refs, groups, block, cap, put):
    spots = lax.broadcasted_iota(jnp.int32, (cap, block), 0).astype(single) + 1.0
    for g in range(groups):
        pick = rank_ref[0, 0, g : g + 1, :] == spots
        pick_b = pick.astype(single).astype(bfloat)
        gate_col = jnp.sum(
            jnp.where(pick, prob_ref[0, 0, g : g + 1, :], 0.0), axis=1, keepdims=True
        )
        entered = dot32(pick_b, rows_of_group(mid_refs, g, groups, ids_ref), ((1,), (0,)))
        cot_row = dot32(pick_b, rows_of_group(cot_refs, g, groups, ids_ref), ((1,), (0,)))
        put(g, entered.astype(bfloat), (cot_row * gate_col).astype(bfloat))


def hidden_and_gradients(x, d, gate, up, down):
    gate_act = dot32(x, gate, ((1,), (0,)))
    up_act = dot32(x, up, ((1,), (0,)))
    sig = 1.0 / (1.0 + jnp.exp(-gate_act))
    silu = gate_act * sig
    hidden = (silu * up_act).astype(bfloat)
    dhidden = dot32(d, down, ((1,), (1,)))
    gate_lin = (dhidden * up_act * sig * (1.0 + gate_act * (1.0 - sig))).astype(bfloat)
    up_lin = (dhidden * silu).astype(bfloat)
    return hidden, gate_lin, up_lin


def cut_of(array, ids_ref, near, far, span):
    parts = [
        array[:, pl.ds(pl.multiple_of((u * near + ids_ref[0]) * span, span), span)]
        for u in range(far)
    ]
    return parts[0] if far == 1 else jnp.concatenate(parts, axis=1)


def own_kernel(
    groups, block, cap, near, far, span, ids_ref, rank_ref, prob_ref, mid_even, mid_odd, cot_even,
    cot_odd, gate_ref, up_ref, down_ref, all_prob_ref, router_ref, hidden_out, gate_out, up_out,
    x_cut, d_cut, moe_even, moe_odd, dmid_even, dmid_odd, dlog_ref, rows_x, rows_d, sum_r, sum_x,
):
    e = pl.program_id(0)
    f = pl.program_id(1)

    @pl.when(f == 0)
    def _():
        def put(g, entered, dreturned):
            rows_x[g * cap : (g + 1) * cap, :] = entered
            rows_d[g * cap : (g + 1) * cap, :] = dreturned

        enter_rows(
            ids_ref, rank_ref, prob_ref, (mid_even, mid_odd), (cot_even, cot_odd), groups, block, cap, put
        )
        x_cut[0] = cut_of(rows_x, ids_ref, near, far, span)
        d_cut[0] = cut_of(rows_d, ids_ref, near, far, span)

    hidden, gate_lin, up_lin = hidden_and_gradients(
        rows_x[...], rows_d[...], gate_ref[0], up_ref[0], down_ref[0]
    )
    hidden_out[0] = hidden
    gate_out[0] = gate_lin
    up_out[0] = up_lin

    def parts():
        r_part = dot32(hidden, down_ref[0], ((1,), (0,)))
        x_part = dot32(gate_lin, gate_ref[0], ((1,), (1,))) + dot32(
            up_lin, up_ref[0], ((1,), (1,))
        )
        return r_part, x_part

    @pl.when(f == 0)
    def _():
        sum_r[...], sum_x[...] = parts()

    @pl.when(f > 0)
    def _():
        r_part, x_part = parts()
        sum_r[...] += r_part
        sum_x[...] += x_part

    @pl.when(f == pl.num_programs(1) - 1)
    def _():
        half = block // 2
        experts = all_prob_ref.shape[1]
        expert_row = lax.broadcasted_iota(jnp.int32, (experts, block), 0)
        spots = lax.broadcasted_iota(jnp.int32, (cap, block), 0).astype(single) + 1.0
        for g in range(groups):
            pick = rank_ref[0, 0, g : g + 1, :] == spots
            pick_f = pick.astype(single)
            pick_b = pick_f.astype(bfloat)
            weighted = (pick_f * prob_ref[0, 0, g : g + 1, :]).astype(bfloat)
            returned = sum_r[g * cap : (g + 1) * cap, :].astype(bfloat)
            cot_row = dot32(
                pick_b, rows_of_group((cot_even, cot_odd), g, groups, ids_ref), ((1,), (0,))
            )
            dgate = jnp.sum(cot_row * returned.astype(single), axis=1, keepdims=True)
            dgate = jnp.sum(jnp.where(pick, dgate, 0.0), axis=0, keepdims=True)
            probs = all_prob_ref[g]
            mine = jnp.where(expert_row == ids_ref[1] + e, dgate, 0.0)
            inner = jnp.sum(probs * mine, axis=0, keepdims=True)
            dlog = probs * (mine - inner)
            moe = dot32(weighted, returned, ((0,), (0,)))
            dmid = dot32(
                pick_b, sum_x[g * cap : (g + 1) * cap, :].astype(bfloat), ((0,), (0,))
            ) + dot32(dlog.astype(bfloat), router_ref[...], ((0,), (0,)))
            rows = slice(g * half, (g + 1) * half)

            @pl.when(e == 0)
            def _():
                dlog_ref[g] = dlog
                moe_even[rows, :] = moe[:half].astype(bfloat)
                moe_odd[rows, :] = moe[half:].astype(bfloat)
                dmid_even[rows, :] = dmid[:half].astype(bfloat)
                dmid_odd[rows, :] = dmid[half:].astype(bfloat)

            @pl.when(e > 0)
            def _():
                dlog_ref[g] += dlog
                for ref, add in (
                    (moe_even, moe[:half]),
                    (moe_odd, moe[half:]),
                    (dmid_even, dmid[:half]),
                    (dmid_odd, dmid[half:]),
                ):
                    ref[rows, :] = (ref[rows, :].astype(single) + add).astype(bfloat)


def others_kernel(
    mids, cots, groups, block, cap, near, far, span, more, ids_ref, rank_ref, prob_ref, *refs
):
    mid_refs, cot_refs, refs = refs[:mids], refs[mids : mids + cots], refs[mids + cots :]
    gate_ref, up_ref, down_ref = refs[:3]
    refs = refs[3:]
    if more:
        own_refs, in_refs, refs = refs[:5], refs[5:8], refs[8:]
    gate_out, up_out, down_out, rows_x, rows_d, hidden_all, gate_all, up_all = refs
    f = pl.program_id(1)
    p = pl.program_id(2)
    height = groups * cap

    @pl.when(f == 0)
    def _():
        def put(g, entered, dreturned):
            rows_x[pl.ds(p * height + g * cap, cap), :] = entered
            rows_d[pl.ds(p * height + g * cap, cap), :] = dreturned

        enter_rows(ids_ref, rank_ref, prob_ref, mid_refs, cot_refs, groups, block, cap, put)

    here = pl.ds(pl.multiple_of(p * height, 16), height)
    hidden, gate_lin, up_lin = hidden_and_gradients(
        rows_x[here, :], rows_d[here, :], gate_ref[0], up_ref[0], down_ref[0]
    )
    hidden_all[here, :] = hidden
    gate_all[here, :] = gate_lin
    up_all[here, :] = up_lin

    @pl.when(p == pl.num_programs(2) - 1)
    def _():
        x_cut = cut_of(rows_x, ids_ref, near, far, span)
        d_cut = cut_of(rows_d, ids_ref, near, far, span)
        gate_part = dot32(x_cut, gate_all[...], ((0,), (0,)))
        up_part = dot32(x_cut, up_all[...], ((0,), (0,)))
        down_part = dot32(hidden_all[...], d_cut, ((0,), (0,)))
        if more:
            x_own, d_own, hidden_own, gate_own, up_own = [ref[0] for ref in own_refs]
            gate_part += in_refs[0][0] + dot32(x_own, gate_own, ((0,), (0,)))
            up_part += in_refs[1][0] + dot32(x_own, up_own, ((0,), (0,)))
            down_part += in_refs[2][0] + dot32(hidden_own, d_own, ((0,), (0,)))
        gate_out[0] = gate_part
        up_out[0] = up_part
        down_out[0] = down_part


vmem = 60 * 1024 * 1024
chunk_units = 512


def routed_own(ids, cap, near, far, rank, prob, mid, cot, gate, up, down, probs, router_t):
    local, _, groups, block = rank.shape
    model = mid[0].shape[-1]
    tokens = groups * block
    units = gate.shape[2]
    chunk = min(chunk_units, units)
    span = model // (near * far)
    own_cols = far * span
    height = groups * cap

    def fixed(shape):
        return pl.BlockSpec(shape, lambda e, f, s: (0,) * len(shape), pipeline_mode=pl.Buffered(1))

    table = pl.BlockSpec((1, 1, groups, block), lambda e, f, s: (e, 0, 0, 0))
    wide = pl.BlockSpec((1, model, chunk), lambda e, f, s: (e, 0, f))
    tall = pl.BlockSpec((1, chunk, model), lambda e, f, s: (e, f, 0))
    lin = pl.BlockSpec((1, height, chunk), lambda e, f, s: (e, 0, f))
    cut = pl.BlockSpec((1, height, own_cols), lambda e, f, s: (e, 0, 0))
    args = [rank, prob, *mid, *cot, gate, up, down, probs, router_t]
    return pl.pallas_call(
        functools.partial(own_kernel, groups, block, cap, near, far, span),
        grid_spec=pltpu.PrefetchScalarGridSpec(
            num_scalar_prefetch=1,
            grid=(local, units // chunk),
            in_specs=[table, table]
            + [fixed(piece.shape) for piece in (*mid, *cot)]
            + [wide, wide, tall, fixed(probs.shape), fixed(router_t.shape)],
            out_specs=[lin] * 3 + [cut] * 2 + [fixed((tokens // 2, model))] * 4 + [fixed(probs.shape)],
            scratch_shapes=[pltpu.VMEM((height, model), bfloat)] * 2
            + [pltpu.VMEM((height, model), single)] * 2,
        ),
        out_shape=[jax.ShapeDtypeStruct((local, height, units), bfloat)] * 3
        + [jax.ShapeDtypeStruct((local, height, own_cols), bfloat)] * 2
        + [jax.ShapeDtypeStruct((tokens // 2, model), bfloat)] * 4
        + [jax.ShapeDtypeStruct(probs.shape, single)],
        compiler_params=pltpu.CompilerParams(
            dimension_semantics=("arbitrary",) * 2, vmem_limit_bytes=vmem
        ),
        cost_estimate=pl.CostEstimate(
            flops=12 * local * height * model * units,
            bytes_accessed=48 << 20,
            transcendentals=height * units,
        ),
        name="routed_own",
    )(ids, *args)


def routed_others(ids, cap, near, far, rank, prob, mid, cot, gate, up, down, more=None):
    local, planes, groups, block = rank.shape
    model = mid.shape[-1]
    units = gate.shape[2]
    chunk = min(chunk_units, units)
    span = model // (near * far)
    own_cols = far * span
    height = groups * cap
    mode = pl.Buffered(1) if planes == 1 else None

    def at_plane(ndim):
        def place(e, f, p, s):
            return (s[2 + jnp.where(f == 0, p, planes - 1)],) + (0,) * (ndim - 1)

        return place

    def rows_spec(piece):
        return pl.BlockSpec((1,) + piece.shape[1:], at_plane(piece.ndim), pipeline_mode=mode)

    table = pl.BlockSpec((1, 1, groups, block), lambda e, f, p, s: (e, p, 0, 0))
    wide = pl.BlockSpec((1, model, chunk), lambda e, f, p, s: (e, 0, f))
    tall = pl.BlockSpec((1, chunk, model), lambda e, f, p, s: (e, f, 0))
    wide_grad = pl.BlockSpec((1, own_cols, chunk), lambda e, f, p, s: (e, 0, f))
    tall_grad = pl.BlockSpec((1, chunk, own_cols), lambda e, f, p, s: (e, f, 0))
    lin = pl.BlockSpec((1, height, chunk), lambda e, f, p, s: (e, 0, f))
    cut = pl.BlockSpec((1, height, own_cols), lambda e, f, p, s: (e, 0, 0))
    in_specs = [table, table] + [rows_spec(piece) for piece in (mid, *cot)] + [wide, wide, tall]
    args = [rank, prob, mid, *cot, gate, up, down]
    aliases = {}
    if more is not None:
        in_specs += [cut, cut, lin, lin, lin, wide_grad, wide_grad, tall_grad]
        args += list(more)
        aliases = {len(args) - 2: 0, len(args) - 1: 1, len(args): 2}
    return pl.pallas_call(
        functools.partial(
            others_kernel, 1, len(cot), groups, block, cap, near, far, span, more is not None
        ),
        grid_spec=pltpu.PrefetchScalarGridSpec(
            num_scalar_prefetch=1,
            grid=(local, units // chunk, planes),
            in_specs=in_specs,
            out_specs=[wide_grad, wide_grad, tall_grad],
            scratch_shapes=[pltpu.VMEM((planes * height, model), bfloat)] * 2
            + [pltpu.VMEM((planes * height, chunk), bfloat)] * 3,
        ),
        out_shape=[
            jax.ShapeDtypeStruct((local, own_cols, units), single),
            jax.ShapeDtypeStruct((local, own_cols, units), single),
            jax.ShapeDtypeStruct((local, units, own_cols), single),
        ],
        input_output_aliases=aliases,
        compiler_params=pltpu.CompilerParams(
            dimension_semantics=("arbitrary",) * 3, vmem_limit_bytes=vmem
        ),
        cost_estimate=pl.CostEstimate(
            flops=8 * local * planes * height * model * units,
            bytes_accessed=64 << 20,
            transcendentals=planes * height * units,
        ),
        name="routed_others",
    )(ids, *args)


def per_device(
    tokens,
    attn_query,
    attn_key,
    attn_value,
    attn_output,
    norm_in,
    norm_query,
    norm_key,
    norm_mid,
    router,
    expert_gate,
    expert_up,
    expert_down,
    routes,
    pieces,
    cotangent,
):
    n = lax.axis_size("expert")
    m = lax.axis_size("dp")
    rows, model = tokens.shape
    shard = attn_query.shape[0]
    experts = router.shape[1]
    top = routes.shape[1]
    local = expert_gate.shape[0]
    length = rows * n
    near = min(m, 4)
    far = m // near
    groups = [[g * near * n + i for i in range(near * n)] for g in range(far)] if far > 1 else None

    def gather_near(values):
        full = lax.all_gather(values, ("dp", "expert"), axis=0, axis_index_groups=groups)
        return full.reshape((near, n) + values.shape)

    half = n // 2
    width = model // n
    heads = width // HEAD
    block = 2 * rows
    mine = lax.axis_index("expert")
    plane = lax.axis_index("dp")
    scale = HEAD ** (-0.5)
    order = slot_order()
    slots = jnp.asarray(order, jnp.int32) ^ mine
    cap = -(-2 * min(rows, rows * top // experts + rows // 32) // 16) * 16

    parts = jnp.stack([attn_query, attn_key, attn_value]).reshape(3, shard, n, width)
    parts_out = parts.transpose(2, 0, 1, 3)
    parts = lax.all_to_all(parts_out, "expert", split_axis=0, concat_axis=0, tiled=True)
    parts = parts.transpose(1, 0, 2, 3).reshape(3, n * shard, width)

    def all_rows(part, first=None):
        held, places = gather_steps(part, "dp", m, first)
        out = []
        for kind in range(part.shape[0]):
            full = jnp.zeros((m, n * shard, width), bfloat)
            for at, kd in enumerate(places):
                full = lax.dynamic_update_slice(
                    full, held[at, kind][None], (plane ^ kd, jnp.int32(0), jnp.int32(0))
                )
            out.append(full.reshape(model, width))
        return out

    first_rows = swap(parts[None, :2], "dp", m - 1)
    x_even, x_odd = gather_halves(after(tokens, parts), first_rows)
    w_q, w_k = all_rows(parts[:2], first_rows)
    cot_even, cot_odd = gather_halves(after(cotangent, x_odd))
    packed = jnp.concatenate(
        [norm_in[None], norm_query[None], norm_key[None], norm_mid[None], router.T], axis=0
    )
    kinds = packed.shape[0]
    packed = jnp.concatenate(
        [
            jnp.pad(packed.reshape(-1), (0, -kinds * shard % HEAD)).reshape(-1, HEAD),
            routes.T.astype(bfloat).reshape(top * rows // HEAD, HEAD),
            pieces.astype(bfloat).reshape(rows // HEAD, HEAD),
        ],
        axis=0,
    )
    packed = after(packed, parts_out)
    small = jnp.stack([packed] + [swap(packed, "dp", mask) for mask in range(1, m)])
    small = jnp.concatenate(gather_halves(small), axis=0)
    cut = -(-kinds * shard // HEAD)
    gains = jnp.take(small[:, :, :cut], jnp.asarray([order.index(j) for j in range(n)]), axis=0)
    gains = jnp.take(gains, jnp.arange(n, dtype=jnp.int32) ^ mine, axis=0)
    gains = jnp.take(gains, jnp.arange(m, dtype=jnp.int32) ^ plane, axis=1)
    gains = gains.reshape(n, m, -1)[:, :, : kinds * shard].reshape(n, m, kinds, shard).transpose(2, 1, 0, 3).reshape(kinds, model)
    gain_in, gain_query, gain_key, gain_mid = [gains[i].astype(single) for i in range(4)]
    router_t = gains[4:]
    piece_row = small[:, 0, cut + top * rows // HEAD :].reshape(length)
    route_rows = small[:, :, cut : cut + top * rows // HEAD].reshape(n, m, top, rows)

    x = jnp.concatenate([x_even, x_odd], axis=0).reshape(length, model).astype(single)
    rs_in = lax.rsqrt(jnp.mean(x * x, axis=-1, keepdims=True) + eps_norm)
    normed_b = (x * rs_in * gain_in).astype(bfloat)
    normed_b = after(normed_b, cot_odd)
    query_raw = dot32(normed_b, w_q, ((1,), (0,)))
    key_raw = dot32(normed_b, w_k, ((1,), (0,)))
    (w_v,) = all_rows(after(parts[2:], w_k, cot_odd))
    near_groups = [[g * near + i for i in range(near)] for g in range(far)] if far > 1 else None
    cot_chunks = [
        lax.all_gather(after(cot_even[place], w_k), "dp", axis=0, axis_index_groups=near_groups)
        for place in range(half)
    ]
    own_shards = []
    send = after(attn_output, w_v)
    for turn in range(m):
        pairs = [(s, ((s % m + turn) % m) * n + s // m) for s in range(m * n)]
        own_shards.append(lax.ppermute(send, ("dp", "expert"), pairs))
    wo = jnp.zeros((m, shard, model), bfloat)
    for turn in range(m):
        wo = lax.dynamic_update_slice(
            wo, own_shards[turn][None], ((plane - turn) % m, jnp.int32(0), jnp.int32(0))
        )
    wo = wo.reshape(width, model)

    squares = jnp.stack([jnp.sum(query_raw**2, axis=-1), jnp.sum(key_raw**2, axis=-1)])
    squares = sum_rows_over_expert(squares.reshape(2, n, rows)).reshape(2, length)
    rs_q = lax.rsqrt(squares[0] / model + eps_norm)[:, None]
    rs_k = lax.rsqrt(squares[1] / model + eps_norm)[:, None]
    value_b = dot32(normed_b, w_v, ((1,), (0,))).astype(bfloat)

    place = (slots[:, None] * rows + jnp.arange(rows, dtype=jnp.int32)[None, :]).reshape(length)
    turn_half = HEAD // 2
    inverse = jnp.exp(jnp.arange(turn_half, dtype=single) * (-2.0 * math.log(rope_base) / HEAD))
    angles = place.astype(single)[:, None] * inverse[None, :]
    cosine = jnp.cos(angles)
    sine = jnp.sin(angles)

    def rotate(values, back):
        out = []
        sn = -sine if back else sine
        for h in range(heads):
            u = values[:, h * HEAD : h * HEAD + turn_half]
            w = values[:, h * HEAD + turn_half : (h + 1) * HEAD]
            out += [u * cosine - w * sn, w * cosine + u * sn]
        return jnp.concatenate(out, axis=-1)

    own_gain_q = lax.dynamic_slice_in_dim(gain_query, mine * width, width)
    own_gain_k = lax.dynamic_slice_in_dim(gain_key, mine * width, width)
    query_b = rotate(query_raw * rs_q * own_gain_q, False).astype(bfloat)
    key_b = rotate(key_raw * rs_k * own_gain_k, False).astype(bfloat)

    def per_head(array):
        return [array[:, h * HEAD : (h + 1) * HEAD] for h in range(heads)]

    allowed = (place[None, :] <= place[:, None]) | (
        (piece_row[:, None] == piece_row[None, :]) & (piece_row[:, None] > 0)
    )
    probs = []
    mixed = []
    for q_h, k_h, v_h in zip(per_head(query_b), per_head(key_b), per_head(value_b)):
        scores = jnp.where(allowed, dot32(q_h, k_h, ((1,), (1,))) * scale, -1e30)
        exponent = jnp.exp(scores - jnp.max(scores, axis=-1, keepdims=True))
        prob = exponent / jnp.sum(exponent, axis=-1, keepdims=True)
        probs.append(prob)
        mixed.append(dot32(prob.astype(bfloat), v_h, ((1,), (0,))))
    attended = jnp.concatenate(mixed, axis=-1).astype(bfloat)

    def halves(array):
        return array[: length // 2], array[length // 2 :]

    projected = [dot32(part, wo, ((1,), (0,))).astype(bfloat) for part in halves(attended)]
    x_own = tokens.astype(single)
    residual = x_own + scatter_sum(*projected)
    rs_mid = lax.rsqrt(jnp.mean(residual * residual, axis=-1, keepdims=True) + eps_norm)
    mid = (residual * rs_mid * gain_mid).astype(bfloat)
    mid_even, mid_odd = gather_halves(mid)
    mid_planes = gather_near(after(mid, mid_odd))

    def router_probs_of(mid_rows):
        logits = dot32(router_t, mid_rows.reshape(-1, model), ((1,), (1,)))
        exponent = jnp.exp(logits - jnp.max(logits, axis=0, keepdims=True))
        return exponent / jnp.sum(exponent, axis=0, keepdims=True)

    upper = (
        jnp.arange(block, dtype=jnp.int32)[:, None] <= jnp.arange(block, dtype=jnp.int32)[None, :]
    ).astype(bfloat)
    ids = (mine * local + jnp.arange(local, dtype=jnp.int32)).astype(bfloat)

    def ranks(kd):
        named = route_rows[:, kd]
        hit = jnp.any(named[None] == ids[:, None, None, None], axis=2)
        hit = jnp.concatenate([hit[:, :half], hit[:, half:]], axis=-1)
        rank = lax.dot_general(
            hit.astype(bfloat), upper, (((2,), (0,)), ((), ())), preferred_element_type=single
        )
        return jnp.where(hit, rank, 0.0)

    def local_probs(array):
        return lax.dynamic_slice_in_dim(array, mine * local, local, 0)

    def grouped(even, odd):
        return jnp.concatenate(
            [even.reshape(-1, half, rows), odd.reshape(-1, half, rows)], axis=-1
        )

    router_probs = grouped(router_probs_of(mid_even), router_probs_of(mid_odd))
    fixed_ids = jnp.stack([plane % near, mine * local])

    def by_group(blocks):
        return jnp.stack([blocks[:half], blocks[half:]], axis=1).reshape(n)

    own_out = routed_own(
        fixed_ids,
        cap,
        near,
        far,
        after(ranks(0)[:, None], cot_chunks[0]),
        local_probs(router_probs)[:, None],
        [mid_even[None], mid_odd[None]],
        [cot_even[None], cot_odd[None]],
        expert_gate,
        expert_up,
        expert_down,
        router_probs.transpose(1, 0, 2),
        router_t,
    )
    hidden_own, gate_lin_own, up_lin_own, x_own_cut, d_own_cut = own_out[:5]
    moe_even, moe_odd, dmid_even, dmid_odd, dlogits = own_out[5:]
    dmid = scatter_sum(dmid_even, after(dmid_odd, cot_chunks[1]))
    scaled = after(dmid, cot_chunks[2]) * gain_mid
    cot_chunks += [swap(after(chunk, dmid), "expert", 1) for chunk in cot_chunks]
    dlogits = dlogits.transpose(1, 0, 2).astype(bfloat)
    router_grad = dot32(
        dlogits[:, :, :rows].reshape(experts, -1), mid_even.reshape(-1, model), ((1,), (0,))
    ) + dot32(dlogits[:, :, rows:].reshape(experts, -1), mid_odd.reshape(-1, model), ((1,), (0,)))

    all_probs = router_probs_of(mid_planes).reshape(experts, near, n, rows)
    all_probs = jnp.take(local_probs(all_probs), by_group(slots), axis=2)

    def add_sequences(masks, more, *earlier):
        planes = [plane % near ^ kd for kd in masks]
        tables = [
            lax.dynamic_index_in_dim(all_probs, there, 1, keepdims=False).reshape(local, half, block)
            for there in planes
        ]
        return routed_others(
            jnp.concatenate([plane[None] % near, jnp.full((1,), len(masks), jnp.int32), jnp.stack(planes), by_group(slots)]),
            cap,
            near,
            far,
            after(jnp.stack([ranks(kd) for kd in masks], axis=1), *earlier),
            jnp.stack(tables, axis=1),
            mid_planes,
            cot_chunks,
            expert_gate,
            expert_up,
            expert_down,
            more,
        )

    mid_grad = jnp.sum(dmid * (residual * rs_mid), axis=0)
    inner = jnp.mean(scaled * residual, axis=-1, keepdims=True)
    dres = cotangent.astype(single) + rs_mid * (scaled - residual * (rs_mid * rs_mid * inner))
    dres_chips = gather_chips(dres.astype(bfloat))
    dres_even = jnp.stack(dres_chips)
    dres_odd = swap(dres_even, "expert", 1).reshape(-1, model)
    dres_even = dres_even.reshape(-1, model)
    datt_b = jnp.concatenate(
        [dot32(part, wo, ((1,), (1,))) for part in (dres_even, dres_odd)], axis=0
    )
    datt_b = after(datt_b, *cot_chunks[3:half]).astype(bfloat)

    moe = scatter_sum(after(moe_even, dres_odd), after(moe_odd, dres_odd))
    output = (residual + moe).astype(bfloat)

    dq_rot, dk_rot, dv = [], [], []
    for prob, da, q_h, k_h, v_h in zip(
        probs, per_head(datt_b), per_head(query_b), per_head(key_b), per_head(value_b)
    ):
        dprob = dot32(da, v_h, ((1,), (1,)))
        dsum = jnp.sum(prob * dprob, axis=-1, keepdims=True)
        dscores = (prob * (dprob - dsum)).astype(bfloat)
        dv.append(dot32(prob.astype(bfloat), da, ((0,), (0,))))
        dq_rot.append(dot32(dscores, k_h, ((1,), (0,))) * scale)
        dk_rot.append(dot32(dscores, q_h, ((0,), (0,))) * scale)
    dq_un = rotate(jnp.concatenate(dq_rot, axis=-1), True)
    dk_un = rotate(jnp.concatenate(dk_rot, axis=-1), True)
    inners = jnp.stack(
        [
            jnp.sum(dq_un * own_gain_q * query_raw, axis=-1),
            jnp.sum(dk_un * own_gain_k * key_raw, axis=-1),
        ]
    )
    inners = after(inners, moe, mid_planes)
    inners = sum_rows_over_expert(inners.reshape(2, n, rows)).reshape(2, length)
    query_gain_grad = jnp.sum(dq_un * query_raw * rs_q, axis=0)
    key_gain_grad = jnp.sum(dk_un * key_raw * rs_k, axis=0)
    dq_b = (
        rs_q * dq_un * own_gain_q - query_raw * (rs_q**3 / model * inners[0][:, None])
    ).astype(bfloat)
    dk_b = (
        rs_k * dk_un * own_gain_k - key_raw * (rs_k**3 / model * inners[1][:, None])
    ).astype(bfloat)
    dv_b = jnp.concatenate(dv, axis=-1).astype(bfloat)
    dnormed_part = [
            (
                dot32(dq_part, w_q, ((1,), (1,)))
                + dot32(dk_part, w_k, ((1,), (1,)))
                + dot32(dv_part, w_v, ((1,), (1,)))
            ).astype(bfloat)
            for dq_part, dk_part, dv_part in zip(halves(dq_b), halves(dk_b), halves(dv_b))
    ]
    dnormed = scatter_sum(*dnormed_part)
    dnormed_part = dnormed_part[0]

    def planes_sum(partials):
        return lax.psum_scatter(
            jnp.stack(partials).astype(bfloat), "dp", scatter_dimension=1, tiled=True
        )

    output_part = dot32(dres_even, attended[: length // 2], ((0,), (0,))) + dot32(
        dres_odd, attended[length // 2 :], ((0,), (0,))
    )
    early = planes_sum([dot32(normed_b, dv_b, ((0,), (0,))), after(output_part, mid_planes)])
    late = planes_sum([dot32(normed_b, part, ((0,), (0,))) for part in (dq_b, dk_b)])
    summed = jnp.concatenate([early[:1], late], axis=0)
    moved = lax.all_to_all(
        summed.reshape(3, n, shard, width).transpose(1, 0, 2, 3),
        "expert",
        split_axis=0,
        concat_axis=0,
        tiled=True,
    )
    moved = moved.transpose(1, 2, 0, 3).reshape(3, shard, model).astype(single)
    value_grad, query_grad, key_grad = moved[0], moved[1], moved[2]
    output_sum = early[1].reshape(model // m, m, shard).transpose(1, 2, 0)
    pieces_here = []
    for turn in range(m):
        pairs = [(((s % m + turn) % m) * n + s // m, s) for s in range(m * n)]
        sent = lax.dynamic_index_in_dim(output_sum, (plane - turn) % m, 0, keepdims=False)
        pieces_here.append(lax.ppermute(sent, ("dp", "expert"), pairs))
    shard_at = (plane * n + mine) % m
    output_grad = jnp.take(
        jnp.stack(pieces_here), (jnp.arange(m, dtype=jnp.int32) - shard_at) % m, axis=0
    )
    output_grad = output_grad.transpose(1, 0, 2).reshape(shard, model).astype(single)

    rs_own = rs_in[:rows]
    scaled_in = dnormed * gain_in
    inner_in = jnp.mean(scaled_in * x_own, axis=-1, keepdims=True)
    input_grad = dres + rs_own * (scaled_in - x_own * (rs_own * rs_own * inner_in))
    in_grad = jnp.sum(dnormed * x_own * rs_own, axis=0)

    def placed(part):
        return lax.dynamic_update_slice(jnp.zeros((model,), single), part, (mine * width,))

    small_grad = jnp.concatenate(
        [
            in_grad[None],
            placed(query_gain_grad)[None],
            placed(key_gain_grad)[None],
            mid_grad[None],
            router_grad,
        ],
        axis=0,
    ).reshape(kinds, m, n, shard)
    small_grad = jnp.take(small_grad, jnp.arange(n, dtype=jnp.int32) ^ mine, axis=2)
    small_pair = small_grad[:, :, 0::2] + swap(small_grad[:, :, 1::2], "expert", 1)
    small_sum = small_pair[:, :, 0]
    for k in range(2, n, 2):
        small_sum = small_sum + swap(small_pair[:, :, k // 2], "expert", k)
    small_sum = jnp.take(small_sum, jnp.arange(m, dtype=jnp.int32) ^ plane, axis=1)
    total = small_sum[:, 0]
    for k in range(1, m):
        total = total + swap(small_sum[:, k], "dp", k)

    weight_sums = add_sequences(list(range(1, near - 1)), None, dnormed_part)
    own_rows = [x_own_cut, d_own_cut, hidden_own, gate_lin_own, up_lin_own]
    weight_sums = add_sequences([near - 1], own_rows + list(weight_sums), dnormed, summed, moved, total)
    gate_grad, up_grad, down_grad = weight_sums
    span = model // m

    def sum_over_far(parts):
        if far == 1:
            return parts[0]
        parts = jnp.take(parts, jnp.arange(far, dtype=jnp.int32) ^ (plane // near), axis=0)
        total = parts[0]
        for k in range(1, far):
            total = total + swap(parts[k].astype(bfloat), "dp", k * near).astype(single)
        return total

    units = expert_gate.shape[2]
    gate_grad, up_grad = [
        sum_over_far(grad.reshape(local, far, span, units).transpose(1, 0, 2, 3))
        for grad in (gate_grad, up_grad)
    ]
    down_grad = sum_over_far(down_grad.reshape(local, units, far, span).transpose(2, 0, 1, 3))

    return (
        output,
        input_grad,
        query_grad,
        key_grad,
        value_grad,
        output_grad,
        total[0],
        total[1],
        total[2],
        total[3],
        total[4:].T,
        gate_grad,
        up_grad,
        down_grad,
    )


def solution(mesh):
    both = ("dp", "expert")
    in_specs = (
        [P(both, None)] * 5
        + [P(both)] * 4
        + [P(both, None)]
        + [P("expert", None, None)] * 3
        + [P(both, None), P(both), P(both, None)]
    )
    out_specs = (
        [P(both, None)] * 6
        + [P(both)] * 4
        + [P(both, None)]
        + [P("expert", "dp", None)] * 2
        + [P("expert", None, "dp")]
    )
    return jax.shard_map(
        per_device,
        mesh=mesh,
        in_specs=tuple(in_specs),
        out_specs=tuple(out_specs),
        check_vma=False,
    )
```

```python
import functools
import math

import jax
import jax.numpy as jnp
from jax import lax
from jax.experimental import pallas as pl
from jax.experimental.pallas import tpu as pltpu
from jax.sharding import PartitionSpec as P

HEAD = 128
eps_norm = 1e-05
rope_base = 10000.0
single = jnp.float32
bfloat = jnp.bfloat16


def dot32(left, right, dims):
    return lax.dot_general(left, right, (dims, ((), ())), preferred_element_type=single)


def after(values, *earlier):
    for result in earlier:
        zero = jnp.minimum(jnp.abs(result[(-1,) * result.ndim]), 0)
        values = values + zero.astype(values.dtype)
    return values


def swap(values, axis, mask):
    count = lax.axis_size(axis)
    return lax.ppermute(values, axis, [(i, i ^ mask) for i in range(count)])


def stage(ready, compute):
    shapes = jax.eval_shape(compute)
    return lax.cond(
        ready, compute, lambda: jax.tree.map(lambda a: jnp.zeros(a.shape, a.dtype), shapes)
    )


def slot_order():
    count = lax.axis_size("expert")
    return list(range(0, count, 2)) + list(range(1, count, 2))


def gather_chips(values):
    count = lax.axis_size("expert")
    return [values if mask == 0 else swap(values, "expert", mask) for mask in range(0, count, 2)]


def gather_halves(values, *earlier):
    even = after(jnp.stack(gather_chips(values)), *earlier)
    return even, swap(even, "expert", 1)


def gather_steps(values, axis, count, first=None):
    held = values[None]
    order = [0]
    mask = count - 1
    while mask > 0:
        other = first if first is not None and mask == count - 1 else swap(held, axis, mask)
        held = jnp.concatenate([held, other], axis=0)
        order = order + [place ^ mask for place in order]
        mask >>= 1
    return held, order


def pair_sums(even, odd):
    half = lax.axis_size("expert") // 2
    rows = even.shape[0] // half
    arrived = swap(odd, "expert", 1)
    parts = [slice(place * rows, (place + 1) * rows) for place in range(half)]
    return [(even[part].astype(single) + arrived[part].astype(single)).astype(bfloat) for part in parts]


def sum_chips(pairs):
    total = pairs[0].astype(single)
    for place in range(1, len(pairs)):
        total = total + swap(pairs[place], "expert", 2 * place).astype(single)
    return total


def scatter_sum(even, odd, with_first=False):
    half = lax.axis_size("expert") // 2
    rows = even.shape[0] // half
    arrived = swap(odd, "expert", 1)
    total = None
    for place in reversed(range(half)):
        part = slice(place * rows, (place + 1) * rows)
        pair = even[part].astype(single) + arrived[part].astype(single)
        if place > 0:
            pair = swap(pair.astype(bfloat), "expert", 2 * place).astype(single)
        if place == half - 1:
            first = arrived
        total = pair if total is None else total + pair
    return (total, first) if with_first else total


def sum_rows_over_expert(values):
    order = slot_order()

    def reorder(array, mask):
        return jnp.concatenate(
            [array[:, order.index(s ^ mask)][:, None] for s in order], axis=1
        )

    total = values + reorder(swap(values, "expert", 1), 1)
    out = total
    for mask in range(2, len(order), 2):
        out = out + reorder(swap(total, "expert", mask), mask)
    return out


def rows_of_group(pieces, g, groups):
    first = len(pieces) // 2
    share = groups // first
    at, part = g // share, g % share
    return jnp.concatenate([pieces[at][0, part], pieces[first + at][0, part]], axis=0)


def enter_rows(ids_ref, rank_ref, prob_ref, mid_refs, cot_refs, groups, block, cap, put):
    spots = lax.broadcasted_iota(jnp.int32, (cap, block), 0).astype(single) + 1.0
    for g in range(groups):
        pick = rank_ref[0, 0, g : g + 1, :] == spots
        pick_b = pick.astype(single).astype(bfloat)
        gate_col = jnp.sum(
            jnp.where(pick, prob_ref[0, 0, g : g + 1, :], 0.0), axis=1, keepdims=True
        )
        entered = dot32(pick_b, rows_of_group(mid_refs, g, groups), ((1,), (0,)))
        cot_row = dot32(pick_b, rows_of_group(cot_refs, g, groups), ((1,), (0,)))
        put(g, entered.astype(bfloat), (cot_row * gate_col).astype(bfloat))


def hidden_and_gradients(x, d, gate, up, down):
    gate_act = dot32(x, gate, ((1,), (0,)))
    up_act = dot32(x, up, ((1,), (0,)))
    sig = 1.0 / (1.0 + jnp.exp(-gate_act))
    silu = gate_act * sig
    hidden = (silu * up_act).astype(bfloat)
    dhidden = dot32(d, down, ((1,), (1,)))
    gate_lin = (dhidden * up_act * sig * (1.0 + gate_act * (1.0 - sig))).astype(bfloat)
    up_lin = (dhidden * silu).astype(bfloat)
    return hidden, gate_lin, up_lin


def cut_of(array, ids_ref, near, far, span):
    parts = [
        array[:, pl.ds(pl.multiple_of((u * near + ids_ref[0]) * span, span), span)]
        for u in range(far)
    ]
    return parts[0] if far == 1 else jnp.concatenate(parts, axis=1)


def own_kernel(
    groups, block, cap, near, far, span, ids_ref, rank_ref, prob_ref, mid_even, mid_odd, cot_even,
    cot_odd, gate_ref, up_ref, down_ref, all_prob_ref, router_ref, hidden_out, gate_out, up_out,
    x_cut, d_cut, moe_even, moe_odd, dmid_even, dmid_odd, dlog_ref, rows_x, rows_d, sum_r, sum_x,
):
    e = pl.program_id(0)
    f = pl.program_id(1)

    @pl.when(f == 0)
    def _():
        def put(g, entered, dreturned):
            rows_x[g * cap : (g + 1) * cap, :] = entered
            rows_d[g * cap : (g + 1) * cap, :] = dreturned

        enter_rows(
            ids_ref, rank_ref, prob_ref, (mid_even, mid_odd), (cot_even, cot_odd), groups, block, cap, put
        )
        x_cut[0] = cut_of(rows_x, ids_ref, near, far, span)
        d_cut[0] = cut_of(rows_d, ids_ref, near, far, span)

    hidden, gate_lin, up_lin = hidden_and_gradients(
        rows_x[...], rows_d[...], gate_ref[0], up_ref[0], down_ref[0]
    )
    hidden_out[0] = hidden
    gate_out[0] = gate_lin
    up_out[0] = up_lin

    def parts():
        r_part = dot32(hidden, down_ref[0], ((1,), (0,)))
        x_part = dot32(gate_lin, gate_ref[0], ((1,), (1,))) + dot32(
            up_lin, up_ref[0], ((1,), (1,))
        )
        return r_part, x_part

    @pl.when(f == 0)
    def _():
        sum_r[...], sum_x[...] = parts()

    @pl.when(f > 0)
    def _():
        r_part, x_part = parts()
        sum_r[...] += r_part
        sum_x[...] += x_part

    @pl.when(f == pl.num_programs(1) - 1)
    def _():
        half = block // 2
        experts = all_prob_ref.shape[1]
        expert_row = lax.broadcasted_iota(jnp.int32, (experts, block), 0)
        spots = lax.broadcasted_iota(jnp.int32, (cap, block), 0).astype(single) + 1.0
        for g in range(groups):
            pick = rank_ref[0, 0, g : g + 1, :] == spots
            pick_f = pick.astype(single)
            pick_b = pick_f.astype(bfloat)
            weighted = (pick_f * prob_ref[0, 0, g : g + 1, :]).astype(bfloat)
            returned = sum_r[g * cap : (g + 1) * cap, :].astype(bfloat)
            cot_row = dot32(
                pick_b, rows_of_group((cot_even, cot_odd), g, groups), ((1,), (0,))
            )
            dgate = jnp.sum(cot_row * returned.astype(single), axis=1, keepdims=True)
            dgate = jnp.sum(jnp.where(pick, dgate, 0.0), axis=0, keepdims=True)
            probs = all_prob_ref[g]
            mine = jnp.where(expert_row == ids_ref[1] + e, dgate, 0.0)
            inner = jnp.sum(probs * mine, axis=0, keepdims=True)
            dlog = probs * (mine - inner)
            moe = dot32(weighted, returned, ((0,), (0,)))
            dmid = dot32(
                pick_b, sum_x[g * cap : (g + 1) * cap, :].astype(bfloat), ((0,), (0,))
            ) + dot32(dlog.astype(bfloat), router_ref[...], ((0,), (0,)))
            rows = slice(g * half, (g + 1) * half)

            @pl.when(e == 0)
            def _():
                dlog_ref[g] = dlog
                moe_even[rows, :] = moe[:half].astype(bfloat)
                moe_odd[rows, :] = moe[half:].astype(bfloat)
                dmid_even[rows, :] = dmid[:half].astype(bfloat)
                dmid_odd[rows, :] = dmid[half:].astype(bfloat)

            @pl.when(e > 0)
            def _():
                dlog_ref[g] += dlog
                for ref, add in (
                    (moe_even, moe[:half]),
                    (moe_odd, moe[half:]),
                    (dmid_even, dmid[:half]),
                    (dmid_odd, dmid[half:]),
                ):
                    ref[rows, :] = (ref[rows, :].astype(single) + add).astype(bfloat)


def others_kernel(
    mids, cots, groups, block, cap, near, far, span, more, ids_ref, rank_ref, prob_ref, *refs
):
    mid_refs, cot_refs, refs = refs[:mids], refs[mids : mids + cots], refs[mids + cots :]
    gate_ref, up_ref, down_ref = refs[:3]
    refs = refs[3:]
    if more:
        own_refs, in_refs, refs = refs[:5], refs[5:8], refs[8:]
    gate_out, up_out, down_out, rows_x, rows_d, hidden_all, gate_all, up_all = refs
    f = pl.program_id(1)
    p = pl.program_id(2)
    height = groups * cap

    @pl.when(f == 0)
    def _():
        def put(g, entered, dreturned):
            rows_x[pl.ds(p * height + g * cap, cap), :] = entered
            rows_d[pl.ds(p * height + g * cap, cap), :] = dreturned

        enter_rows(ids_ref, rank_ref, prob_ref, mid_refs, cot_refs, groups, block, cap, put)

    here = pl.ds(pl.multiple_of(p * height, 16), height)
    hidden, gate_lin, up_lin = hidden_and_gradients(
        rows_x[here, :], rows_d[here, :], gate_ref[0], up_ref[0], down_ref[0]
    )
    hidden_all[here, :] = hidden
    gate_all[here, :] = gate_lin
    up_all[here, :] = up_lin

    @pl.when(p == pl.num_programs(2) - 1)
    def _():
        x_cut = cut_of(rows_x, ids_ref, near, far, span)
        d_cut = cut_of(rows_d, ids_ref, near, far, span)
        gate_part = dot32(x_cut, gate_all[...], ((0,), (0,)))
        up_part = dot32(x_cut, up_all[...], ((0,), (0,)))
        down_part = dot32(hidden_all[...], d_cut, ((0,), (0,)))
        if more:
            x_own, d_own, hidden_own, gate_own, up_own = [ref[0] for ref in own_refs]
            gate_part += in_refs[0][0] + dot32(x_own, gate_own, ((0,), (0,)))
            up_part += in_refs[1][0] + dot32(x_own, up_own, ((0,), (0,)))
            down_part += in_refs[2][0] + dot32(hidden_own, d_own, ((0,), (0,)))
        gate_out[0] = gate_part
        up_out[0] = up_part
        down_out[0] = down_part


vmem = 60 * 1024 * 1024
chunk_units = 512


def routed_own(ids, cap, near, far, rank, prob, mid, cot, gate, up, down, probs, router_t):
    local, _, groups, block = rank.shape
    model = mid[0].shape[-1]
    tokens = groups * block
    units = gate.shape[2]
    chunk = min(chunk_units, units)
    span = model // (near * far)
    own_cols = far * span
    height = groups * cap

    def fixed(shape):
        return pl.BlockSpec(shape, lambda e, f, s: (0,) * len(shape), pipeline_mode=pl.Buffered(1))

    table = pl.BlockSpec((1, 1, groups, block), lambda e, f, s: (e, 0, 0, 0))
    wide = pl.BlockSpec((1, model, chunk), lambda e, f, s: (e, 0, f))
    tall = pl.BlockSpec((1, chunk, model), lambda e, f, s: (e, f, 0))
    lin = pl.BlockSpec((1, height, chunk), lambda e, f, s: (e, 0, f))
    cut = pl.BlockSpec((1, height, own_cols), lambda e, f, s: (e, 0, 0))
    args = [rank, prob, *mid, *cot, gate, up, down, probs, router_t]
    return pl.pallas_call(
        functools.partial(own_kernel, groups, block, cap, near, far, span),
        grid_spec=pltpu.PrefetchScalarGridSpec(
            num_scalar_prefetch=1,
            grid=(local, units // chunk),
            in_specs=[table, table]
            + [fixed(piece.shape) for piece in (*mid, *cot)]
            + [wide, wide, tall, fixed(probs.shape), fixed(router_t.shape)],
            out_specs=[lin] * 3 + [cut] * 2 + [fixed((tokens // 2, model))] * 4 + [fixed(probs.shape)],
            scratch_shapes=[pltpu.VMEM((height, model), bfloat)] * 2
            + [pltpu.VMEM((height, model), single)] * 2,
        ),
        out_shape=[jax.ShapeDtypeStruct((local, height, units), bfloat)] * 3
        + [jax.ShapeDtypeStruct((local, height, own_cols), bfloat)] * 2
        + [jax.ShapeDtypeStruct((tokens // 2, model), bfloat)] * 4
        + [jax.ShapeDtypeStruct(probs.shape, single)],
        compiler_params=pltpu.CompilerParams(
            dimension_semantics=("arbitrary",) * 2, vmem_limit_bytes=vmem
        ),
        cost_estimate=pl.CostEstimate(
            flops=12 * local * height * model * units,
            bytes_accessed=48 << 20,
            transcendentals=height * units,
        ),
        name="routed_own",
    )(ids, *args)


def routed_others(ids, cap, near, far, rank, prob, mid, cot, gate, up, down, more=None):
    local, planes, groups, block = rank.shape
    model = mid[0].shape[-1]
    units = gate.shape[2]
    chunk = min(chunk_units, units)
    span = model // (near * far)
    own_cols = far * span
    height = groups * cap
    mode = pl.Buffered(1) if planes == 1 else None

    def at_plane(ndim):
        def place(e, f, p, s):
            return (s[2 + jnp.where(f == 0, p, planes - 1)],) + (0,) * (ndim - 1)

        return place

    def rows_spec(piece):
        return pl.BlockSpec((1,) + piece.shape[1:], at_plane(piece.ndim), pipeline_mode=mode)

    table = pl.BlockSpec((1, 1, groups, block), lambda e, f, p, s: (e, p, 0, 0))
    wide = pl.BlockSpec((1, model, chunk), lambda e, f, p, s: (e, 0, f))
    tall = pl.BlockSpec((1, chunk, model), lambda e, f, p, s: (e, f, 0))
    wide_grad = pl.BlockSpec((1, own_cols, chunk), lambda e, f, p, s: (e, 0, f))
    tall_grad = pl.BlockSpec((1, chunk, own_cols), lambda e, f, p, s: (e, f, 0))
    lin = pl.BlockSpec((1, height, chunk), lambda e, f, p, s: (e, 0, f))
    cut = pl.BlockSpec((1, height, own_cols), lambda e, f, p, s: (e, 0, 0))
    in_specs = [table, table] + [rows_spec(piece) for piece in (*mid, *cot)] + [wide, wide, tall]
    args = [rank, prob, *mid, *cot, gate, up, down]
    aliases = {}
    if more is not None:
        in_specs += [cut, cut, lin, lin, lin, wide_grad, wide_grad, tall_grad]
        args += list(more)
        aliases = {len(args) - 2: 0, len(args) - 1: 1, len(args): 2}
    return pl.pallas_call(
        functools.partial(
            others_kernel, len(mid), len(cot), groups, block, cap, near, far, span, more is not None
        ),
        grid_spec=pltpu.PrefetchScalarGridSpec(
            num_scalar_prefetch=1,
            grid=(local, units // chunk, planes),
            in_specs=in_specs,
            out_specs=[wide_grad, wide_grad, tall_grad],
            scratch_shapes=[pltpu.VMEM((planes * height, model), bfloat)] * 2
            + [pltpu.VMEM((planes * height, chunk), bfloat)] * 3,
        ),
        out_shape=[
            jax.ShapeDtypeStruct((local, own_cols, units), single),
            jax.ShapeDtypeStruct((local, own_cols, units), single),
            jax.ShapeDtypeStruct((local, units, own_cols), single),
        ],
        input_output_aliases=aliases,
        compiler_params=pltpu.CompilerParams(
            dimension_semantics=("arbitrary",) * 3, vmem_limit_bytes=vmem
        ),
        cost_estimate=pl.CostEstimate(
            flops=8 * local * planes * height * model * units,
            bytes_accessed=64 << 20,
            transcendentals=planes * height * units,
        ),
        name="routed_others",
    )(ids, *args)


def per_device(
    tokens,
    attn_query,
    attn_key,
    attn_value,
    attn_output,
    norm_in,
    norm_query,
    norm_key,
    norm_mid,
    router,
    expert_gate,
    expert_up,
    expert_down,
    routes,
    pieces,
    cotangent,
):
    n = lax.axis_size("expert")
    m = lax.axis_size("dp")
    rows, model = tokens.shape
    shard = attn_query.shape[0]
    experts = router.shape[1]
    top = routes.shape[1]
    local = expert_gate.shape[0]
    length = rows * n
    near = min(m, 4)
    far = m // near
    half = n // 2
    width = model // n
    heads = width // HEAD
    block = 2 * rows
    mine = lax.axis_index("expert")
    plane = lax.axis_index("dp")
    ready = routes[0, 0] >= 0
    scale = HEAD ** (-0.5)
    order = slot_order()
    slots = jnp.asarray(order, jnp.int32) ^ mine
    cap = -(-2 * min(rows, rows * top // experts + rows // 32) // 16) * 16

    parts = jnp.stack([attn_query, attn_key, attn_value]).reshape(3, shard, n, width)
    parts_out = parts.transpose(2, 0, 1, 3)
    parts = lax.all_to_all(parts_out, "expert", split_axis=0, concat_axis=0, tiled=True)
    parts = parts.transpose(1, 0, 2, 3).reshape(3, n * shard, width)

    def all_rows(part, first=None):
        held, places = gather_steps(part, "dp", m, first)
        out = []
        for kind in range(part.shape[0]):
            full = jnp.zeros((m, n * shard, width), bfloat)
            for at, kd in enumerate(places):
                full = lax.dynamic_update_slice(
                    full, held[at, kind][None], (plane ^ kd, jnp.int32(0), jnp.int32(0))
                )
            out.append(full.reshape(model, width))
        return out

    packed = jnp.concatenate(
        [norm_in[None], norm_query[None], norm_key[None], norm_mid[None], router.T], axis=0
    )
    kinds = packed.shape[0]
    packed = jnp.concatenate(
        [
            jnp.pad(packed.reshape(-1), (0, -kinds * shard % HEAD)).reshape(-1, HEAD),
            routes.T.astype(bfloat).reshape(top * rows // HEAD, HEAD),
            pieces.astype(bfloat).reshape(rows // HEAD, HEAD),
        ],
        axis=0,
    )
    packed = after(packed, parts_out)
    small, places = gather_steps(packed, "dp", m)
    first_rows = swap(after(parts[None], small), "dp", m - 1)
    small = jnp.stack([small[places.index(kd)] for kd in range(m)])
    small = jnp.concatenate(gather_halves(small), axis=0)
    chips = gather_chips(after(jnp.stack([tokens, cotangent]), parts))
    x_even = after(jnp.stack([piece[0] for piece in chips]), first_rows)
    x_odd = swap(x_even, "expert", 1)
    cot_even = jnp.stack([piece[1] for piece in chips])
    cot_odd = swap(cot_even, "expert", 1)
    w_q, w_k, w_v = all_rows(parts, first_rows)
    cut = -(-kinds * shard // HEAD)
    gains = jnp.take(small[:, :, :cut], jnp.asarray([order.index(j) for j in range(n)]), axis=0)
    gains = jnp.take(gains, jnp.arange(n, dtype=jnp.int32) ^ mine, axis=0)
    gains = jnp.take(gains, jnp.arange(m, dtype=jnp.int32) ^ plane, axis=1)
    gains = gains.reshape(n, m, -1)[:, :, : kinds * shard].reshape(n, m, kinds, shard).transpose(2, 1, 0, 3).reshape(kinds, model)
    gain_in, gain_query, gain_key, gain_mid = [gains[i].astype(single) for i in range(4)]
    router_t = gains[4:]
    piece_row = small[:, 0, cut + top * rows // HEAD :].reshape(length)
    route_rows = small[:, :, cut : cut + top * rows // HEAD].reshape(n, m, top, rows)

    x = jnp.concatenate([x_even, x_odd], axis=0).reshape(length, model).astype(single)
    rs_in = lax.rsqrt(jnp.mean(x * x, axis=-1, keepdims=True) + eps_norm)
    normed_b = (x * rs_in * gain_in).astype(bfloat)

    near_groups = [[g * near + i for i in range(near)] for g in range(far)] if far > 1 else None
    cot_planes = lax.all_gather(after(cot_even, w_v), "dp", axis=0, axis_index_groups=near_groups)

    place = (slots[:, None] * rows + jnp.arange(rows, dtype=jnp.int32)[None, :]).reshape(length)
    turn_half = HEAD // 2
    inverse = jnp.exp(jnp.arange(turn_half, dtype=single) * (-2.0 * math.log(rope_base) / HEAD))
    angles = place.astype(single)[:, None] * inverse[None, :]
    cosine = jnp.cos(angles)
    sine = jnp.sin(angles)

    def rotate(values, back):
        out = []
        sn = -sine if back else sine
        for h in range(heads):
            u = values[:, h * HEAD : h * HEAD + turn_half]
            w = values[:, h * HEAD + turn_half : (h + 1) * HEAD]
            out += [u * cosine - w * sn, w * cosine + u * sn]
        return jnp.concatenate(out, axis=-1)

    own_gain_q = lax.dynamic_slice_in_dim(gain_query, mine * width, width)
    own_gain_k = lax.dynamic_slice_in_dim(gain_key, mine * width, width)
    def per_head(array):
        return [array[:, h * HEAD : (h + 1) * HEAD] for h in range(heads)]

    def halves(array):
        return array[: length // 2], array[length // 2 :]

    upper = (
        jnp.arange(block, dtype=jnp.int32)[:, None] <= jnp.arange(block, dtype=jnp.int32)[None, :]
    ).astype(bfloat)
    ids = (mine * local + jnp.arange(local, dtype=jnp.int32)).astype(bfloat)

    def ranks(kd):
        named = route_rows[:, kd]
        hit = jnp.any(named[None] == ids[:, None, None, None], axis=2)
        hit = jnp.concatenate([hit[:, :half], hit[:, half:]], axis=-1)
        rank = lax.dot_general(
            hit.astype(bfloat), upper, (((2,), (0,)), ((), ())), preferred_element_type=single
        )
        return jnp.where(hit, rank, 0.0)

    own_ranks = after(ranks(0)[:, None], cot_odd)

    x_own = tokens.astype(single)

    def forward():
        query_raw = dot32(normed_b, w_q, ((1,), (0,)))
        key_raw = dot32(normed_b, w_k, ((1,), (0,)))
        own_shards = []
        send = attn_output
        for turn in range(m):
            pairs = [(s, ((s % m + turn) % m) * n + s // m) for s in range(m * n)]
            own_shards.append(lax.ppermute(send, ("dp", "expert"), pairs))
        wo = jnp.zeros((m, shard, model), bfloat)
        for turn in range(m):
            wo = lax.dynamic_update_slice(
                wo, own_shards[turn][None], ((plane - turn) % m, jnp.int32(0), jnp.int32(0))
            )
        wo = wo.reshape(width, model)

        squares = jnp.stack([jnp.sum(query_raw**2, axis=-1), jnp.sum(key_raw**2, axis=-1)])
        squares = sum_rows_over_expert(squares.reshape(2, n, rows)).reshape(2, length)
        rs_q = lax.rsqrt(squares[0] / model + eps_norm)[:, None]
        rs_k = lax.rsqrt(squares[1] / model + eps_norm)[:, None]
        value_b = dot32(normed_b, w_v, ((1,), (0,))).astype(bfloat)

        query_b = rotate(query_raw * rs_q * own_gain_q, False).astype(bfloat)
        key_b = rotate(key_raw * rs_k * own_gain_k, False).astype(bfloat)

        allowed = (place[None, :] <= place[:, None]) | (
            (piece_row[:, None] == piece_row[None, :]) & (piece_row[:, None] > 0)
        )
        probs = []
        mixed = []
        for q_h, k_h, v_h in zip(per_head(query_b), per_head(key_b), per_head(value_b)):
            scores = jnp.where(allowed, dot32(q_h, k_h, ((1,), (1,))) * scale, -1e30)
            exponent = jnp.exp(scores - jnp.max(scores, axis=-1, keepdims=True))
            prob = exponent / jnp.sum(exponent, axis=-1, keepdims=True)
            probs.append(prob)
            mixed.append(dot32(prob.astype(bfloat), v_h, ((1,), (0,))))
        attended = jnp.concatenate(mixed, axis=-1).astype(bfloat)

        projected = [dot32(part, wo, ((1,), (0,))).astype(bfloat) for part in halves(attended)]
        residual = x_own + scatter_sum(*projected)
        rs_mid = lax.rsqrt(jnp.mean(residual * residual, axis=-1, keepdims=True) + eps_norm)
        mid = after(residual * rs_mid * gain_mid, own_ranks).astype(bfloat)
        mid_even, mid_odd = gather_halves(mid)
        kept = (query_raw, key_raw, rs_q, rs_k, query_b, key_b, value_b, wo)
        return kept, probs, attended, residual, rs_mid, mid_even, mid_odd

    kept, probs, attended, residual, rs_mid, mid_even, mid_odd = stage(ready, forward)
    query_raw, key_raw, rs_q, rs_k, query_b, key_b, value_b, wo = kept
    mid_planes = lax.all_gather(after(mid_even, cot_planes), "dp", axis=0, axis_index_groups=near_groups)

    def router_probs_of(mid_rows):
        logits = dot32(router_t, mid_rows.reshape(-1, model), ((1,), (1,)))
        exponent = jnp.exp(logits - jnp.max(logits, axis=0, keepdims=True))
        return exponent / jnp.sum(exponent, axis=0, keepdims=True)

    def local_probs(array):
        return lax.dynamic_slice_in_dim(array, mine * local, local, 0)

    def grouped(even, odd):
        return jnp.concatenate(
            [even.reshape(-1, half, rows), odd.reshape(-1, half, rows)], axis=-1
        )

    router_probs = grouped(router_probs_of(mid_even), router_probs_of(mid_odd))
    fixed_ids = jnp.stack([plane % near, mine * local])

    def by_group(blocks):
        return jnp.stack([blocks[:half], blocks[half:]], axis=1).reshape(n)

    def backward():
        own_out = routed_own(
            fixed_ids,
            cap,
            near,
            far,
            own_ranks,
            local_probs(router_probs)[:, None],
            [mid_even[None], mid_odd[None]],
            [cot_even[None], cot_odd[None]],
            expert_gate,
            expert_up,
            expert_down,
            router_probs.transpose(1, 0, 2),
            router_t,
        )
        hidden_own, gate_lin_own, up_lin_own, x_own_cut, d_own_cut = own_out[:5]
        moe_even, moe_odd, dmid_even, dmid_odd, dlogits = own_out[5:]
        dmid = scatter_sum(dmid_even, dmid_odd)
        scaled = dmid * gain_mid
        mid_grad = jnp.sum(dmid * (residual * rs_mid), axis=0)
        inner = jnp.mean(scaled * residual, axis=-1, keepdims=True)
        dres = cotangent.astype(single) + rs_mid * (scaled - residual * (rs_mid * rs_mid * inner))
        dres_chips = gather_chips(dres.astype(bfloat))
        dres_even = jnp.stack(dres_chips)
        dres_odd = swap(dres_even, "expert", 1).reshape(-1, model)
        dres_even = dres_even.reshape(-1, model)
        datt_b = jnp.concatenate(
            [dot32(part, wo, ((1,), (1,))) for part in (dres_even, dres_odd)], axis=0
        )
        datt_b = datt_b.astype(bfloat)

        moe_pairs = pair_sums(after(moe_even, dres_odd), after(moe_odd, dres_odd))
        cot_planes_odd = swap(cot_planes, "expert", 1)
        gate_tables = [swap(local_probs(router_probs), "dp", kd) for kd in range(1, near)]

        dq_rot, dk_rot, dv = [], [], []
        for prob, da, q_h, k_h, v_h in zip(
            probs, per_head(datt_b), per_head(query_b), per_head(key_b), per_head(value_b)
        ):
            dprob = dot32(da, v_h, ((1,), (1,)))
            dsum = jnp.sum(prob * dprob, axis=-1, keepdims=True)
            dscores = (prob * (dprob - dsum)).astype(bfloat)
            dv.append(dot32(prob.astype(bfloat), da, ((0,), (0,))))
            dq_rot.append(dot32(dscores, k_h, ((1,), (0,))) * scale)
            dk_rot.append(dot32(dscores, q_h, ((0,), (0,))) * scale)
        dq_un = rotate(jnp.concatenate(dq_rot, axis=-1), True)
        dk_un = rotate(jnp.concatenate(dk_rot, axis=-1), True)
        inners = jnp.stack(
            [
                jnp.sum(dq_un * own_gain_q * query_raw, axis=-1),
                jnp.sum(dk_un * own_gain_k * key_raw, axis=-1),
            ]
        )
        inners = sum_rows_over_expert(inners.reshape(2, n, rows)).reshape(2, length)
        query_gain_grad = jnp.sum(dq_un * query_raw * rs_q, axis=0)
        key_gain_grad = jnp.sum(dk_un * key_raw * rs_k, axis=0)
        dq_b = (
            rs_q * dq_un * own_gain_q - query_raw * (rs_q**3 / model * inners[0][:, None])
        ).astype(bfloat)
        dk_b = (
            rs_k * dk_un * own_gain_k - key_raw * (rs_k**3 / model * inners[1][:, None])
        ).astype(bfloat)
        dv_b = jnp.concatenate(dv, axis=-1).astype(bfloat)
        dnormed_part = [
                (
                    dot32(dq_part, w_q, ((1,), (1,)))
                    + dot32(dk_part, w_k, ((1,), (1,)))
                    + dot32(dv_part, w_v, ((1,), (1,)))
                ).astype(bfloat)
                for dq_part, dk_part, dv_part in zip(halves(dq_b), halves(dk_b), halves(dv_b))
        ]
        output_part = dot32(dres_even, attended[: length // 2], ((0,), (0,))) + dot32(
            dres_odd, attended[length // 2 :], ((0,), (0,))
        )
        early = jnp.stack([dot32(normed_b, dv_b, ((0,), (0,))), output_part]).astype(bfloat)
        late = jnp.stack([dot32(normed_b, part, ((0,), (0,))) for part in (dq_b, dk_b)])
        late = late.astype(bfloat)
        return (
            own_out,
            dres,
            dres_even,
            dres_odd,
            mid_grad,
            query_gain_grad,
            key_gain_grad,
            dq_b,
            dk_b,
            dv_b,
            dnormed_part,
            moe_pairs,
            cot_planes_odd,
            gate_tables,
            early,
            late,
        )

    (
        own_out,
        dres,
        dres_even,
        dres_odd,
        mid_grad,
        query_gain_grad,
        key_gain_grad,
        dq_b,
        dk_b,
        dv_b,
        dnormed_part,
        moe_pairs,
        cot_planes_odd,
        gate_tables,
        early,
        late,
    ) = stage(ready, backward)
    hidden_own, gate_lin_own, up_lin_own, x_own_cut, d_own_cut = own_out[:5]
    moe_even, moe_odd, dmid_even, dmid_odd, dlogits = own_out[5:]
    dnormed = scatter_sum(*dnormed_part)
    dnormed_part = dnormed_part[0]

    dlogits = dlogits.transpose(1, 0, 2).astype(bfloat)
    router_grad = dot32(
        dlogits[:, :, :rows].reshape(experts, -1), mid_even.reshape(-1, model), ((1,), (0,))
    ) + dot32(dlogits[:, :, rows:].reshape(experts, -1), mid_odd.reshape(-1, model), ((1,), (0,)))

    mid_planes = [mid_planes, swap(mid_planes, "expert", 1)]
    cot_planes = [cot_planes, cot_planes_odd]
    def add_sequences(masks, more, *earlier):
        planes = [plane % near ^ kd for kd in masks]
        return routed_others(
            jnp.concatenate([plane[None] % near, jnp.full((1,), len(masks), jnp.int32), jnp.stack(planes)]),
            cap,
            near,
            far,
            after(jnp.stack([ranks(kd) for kd in masks], axis=1), *earlier),
            jnp.stack([gate_tables[kd - 1] for kd in masks], axis=1),
            mid_planes,
            cot_planes,
            expert_gate,
            expert_up,
            expert_down,
            more,
        )

    late = lax.psum_scatter(late, "dp", scatter_dimension=1, tiled=True)
    early = lax.psum_scatter(early, "dp", scatter_dimension=1, tiled=True)
    moe = sum_chips(moe_pairs)
    weight_sums = add_sequences(list(range(1, near - 1)), None, dnormed_part)
    dnormed = after(dnormed, weight_sums[0])
    summed = jnp.concatenate([early[:1], late], axis=0)
    moved = lax.all_to_all(
        after(summed, weight_sums[0]).reshape(3, n, shard, width).transpose(1, 0, 2, 3),
        "expert",
        split_axis=0,
        concat_axis=0,
        tiled=True,
    )
    moved = moved.transpose(1, 2, 0, 3).reshape(3, shard, model).astype(single)
    value_grad, query_grad, key_grad = moved[0], moved[1], moved[2]
    output_sum = after(early[1], weight_sums[0]).reshape(model // m, m, shard).transpose(1, 2, 0)
    pieces_here = []
    for turn in range(m):
        pairs = [(((s % m + turn) % m) * n + s // m, s) for s in range(m * n)]
        sent = lax.dynamic_index_in_dim(output_sum, (plane - turn) % m, 0, keepdims=False)
        pieces_here.append(lax.ppermute(sent, ("dp", "expert"), pairs))
    shard_at = (plane * n + mine) % m
    output_grad = jnp.take(
        jnp.stack(pieces_here), (jnp.arange(m, dtype=jnp.int32) - shard_at) % m, axis=0
    )
    output_grad = output_grad.transpose(1, 0, 2).reshape(shard, model).astype(single)

    output = (residual + moe).astype(bfloat)
    rs_own = rs_in[:rows]
    scaled_in = dnormed * gain_in
    inner_in = jnp.mean(scaled_in * x_own, axis=-1, keepdims=True)
    input_grad = dres + rs_own * (scaled_in - x_own * (rs_own * rs_own * inner_in))
    in_grad = jnp.sum(dnormed * x_own * rs_own, axis=0)

    def placed(part):
        return lax.dynamic_update_slice(jnp.zeros((model,), single), part, (mine * width,))

    small_grad = jnp.concatenate(
        [
            in_grad[None],
            placed(query_gain_grad)[None],
            placed(key_gain_grad)[None],
            mid_grad[None],
            router_grad,
        ],
        axis=0,
    ).reshape(kinds, m, n, shard)
    small_grad = jnp.take(small_grad, jnp.arange(n, dtype=jnp.int32) ^ mine, axis=2)
    small_pair = small_grad[:, :, 0::2] + swap(small_grad[:, :, 1::2], "expert", 1)
    small_sum = small_pair[:, :, 0]
    for k in range(2, n, 2):
        small_sum = small_sum + swap(small_pair[:, :, k // 2], "expert", k)
    small_sum = jnp.take(small_sum, jnp.arange(m, dtype=jnp.int32) ^ plane, axis=1)
    total = small_sum[:, 0]
    for k in range(1, m):
        total = total + swap(small_sum[:, k], "dp", k)

    own_rows = [x_own_cut, d_own_cut, hidden_own, gate_lin_own, up_lin_own]
    weight_sums = add_sequences([near - 1], own_rows + list(weight_sums), moe)
    gate_grad, up_grad, down_grad = weight_sums
    span = model // m

    def sum_over_far(parts):
        if far == 1:
            return parts[0]
        parts = jnp.take(parts, jnp.arange(far, dtype=jnp.int32) ^ (plane // near), axis=0)
        total = parts[0]
        for k in range(1, far):
            total = total + swap(parts[k].astype(bfloat), "dp", k * near).astype(single)
        return total

    units = expert_gate.shape[2]
    gate_grad, up_grad = [
        sum_over_far(grad.reshape(local, far, span, units).transpose(1, 0, 2, 3))
        for grad in (gate_grad, up_grad)
    ]
    down_grad = sum_over_far(down_grad.reshape(local, units, far, span).transpose(2, 0, 1, 3))

    return (
        output,
        input_grad,
        query_grad,
        key_grad,
        value_grad,
        output_grad,
        total[0],
        total[1],
        total[2],
        total[3],
        total[4:].T,
        gate_grad,
        up_grad,
        down_grad,
    )


def solution(mesh):
    both = ("dp", "expert")
    in_specs = (
        [P(both, None)] * 5
        + [P(both)] * 4
        + [P(both, None)]
        + [P("expert", None, None)] * 3
        + [P(both, None), P(both), P(both, None)]
    )
    out_specs = (
        [P(both, None)] * 6
        + [P(both)] * 4
        + [P(both, None)]
        + [P("expert", "dp", None)] * 2
        + [P("expert", None, "dp")]
    )
    return jax.shard_map(
        per_device,
        mesh=mesh,
        in_specs=tuple(in_specs),
        out_specs=tuple(out_specs),
        check_vma=False,
    )
```

```python
import functools
import math

import jax
import jax.numpy as jnp
from jax import lax
from jax.experimental import pallas as pl
from jax.experimental.pallas import tpu as pltpu
from jax.sharding import PartitionSpec as P

HEAD = 128
eps_norm = 1e-05
rope_base = 10000.0
single = jnp.float32
bfloat = jnp.bfloat16


def dot32(left, right, dims):
    return lax.dot_general(left, right, (dims, ((), ())), preferred_element_type=single)


def after(values, *earlier):
    for result in earlier:
        zero = jnp.minimum(jnp.abs(result[(-1,) * result.ndim]), 0)
        values = values + zero.astype(values.dtype)
    return values


def swap(values, axis, mask):
    count = lax.axis_size(axis)
    return lax.ppermute(values, axis, [(i, i ^ mask) for i in range(count)])


def stage(ready, compute):
    shapes = jax.eval_shape(compute)
    return lax.cond(
        ready, compute, lambda: jax.tree.map(lambda a: jnp.zeros(a.shape, a.dtype), shapes)
    )


def slot_order():
    count = lax.axis_size("expert")
    return list(range(0, count, 2)) + list(range(1, count, 2))


def gather_chips(values):
    count = lax.axis_size("expert")
    return [values if mask == 0 else swap(values, "expert", mask) for mask in range(0, count, 2)]


def gather_halves(values, *earlier):
    even = after(jnp.stack(gather_chips(values)), *earlier)
    return even, swap(even, "expert", 1)


def gather_steps(values, axis, count, first=None):
    held = values[None]
    order = [0]
    mask = count - 1
    while mask > 0:
        other = first if first is not None and mask == count - 1 else swap(held, axis, mask)
        held = jnp.concatenate([held, other], axis=0)
        order = order + [place ^ mask for place in order]
        mask >>= 1
    return held, order


def pair_sums(even, odd):
    half = lax.axis_size("expert") // 2
    rows = even.shape[0] // half
    arrived = swap(odd, "expert", 1)
    parts = [slice(place * rows, (place + 1) * rows) for place in range(half)]
    return [(even[part].astype(single) + arrived[part].astype(single)).astype(bfloat) for part in parts]


def sum_chips(pairs):
    total = pairs[0].astype(single)
    for place in range(1, len(pairs)):
        total = total + swap(pairs[place], "expert", 2 * place).astype(single)
    return total


def scatter_sum(even, odd, with_first=False):
    half = lax.axis_size("expert") // 2
    rows = even.shape[0] // half
    arrived = swap(odd, "expert", 1)
    total = None
    for place in reversed(range(half)):
        part = slice(place * rows, (place + 1) * rows)
        pair = even[part].astype(single) + arrived[part].astype(single)
        if place > 0:
            pair = swap(pair.astype(bfloat), "expert", 2 * place).astype(single)
        if place == half - 1:
            first = arrived
        total = pair if total is None else total + pair
    return (total, first) if with_first else total


def sum_rows_over_expert(values):
    order = slot_order()

    def reorder(array, mask):
        return jnp.concatenate(
            [array[:, order.index(s ^ mask)][:, None] for s in order], axis=1
        )

    total = values + reorder(swap(values, "expert", 1), 1)
    out = total
    for mask in range(2, len(order), 2):
        out = out + reorder(swap(total, "expert", mask), mask)
    return out


def rows_of_group(pieces, g, groups):
    first = len(pieces) // 2
    share = groups // first
    at, part = g // share, g % share
    return jnp.concatenate([pieces[at][0, part], pieces[first + at][0, part]], axis=0)


def enter_rows(ids_ref, rank_ref, prob_ref, mid_refs, cot_refs, groups, block, cap, put):
    spots = lax.broadcasted_iota(jnp.int32, (cap, block), 0).astype(single) + 1.0
    for g in range(groups):
        pick = rank_ref[0, 0, g : g + 1, :] == spots
        pick_b = pick.astype(single).astype(bfloat)
        gate_col = jnp.sum(
            jnp.where(pick, prob_ref[0, 0, g : g + 1, :], 0.0), axis=1, keepdims=True
        )
        entered = dot32(pick_b, rows_of_group(mid_refs, g, groups), ((1,), (0,)))
        cot_row = dot32(pick_b, rows_of_group(cot_refs, g, groups), ((1,), (0,)))
        put(g, entered.astype(bfloat), (cot_row * gate_col).astype(bfloat))


def hidden_and_gradients(x, d, gate, up, down):
    gate_act = dot32(x, gate, ((1,), (0,)))
    up_act = dot32(x, up, ((1,), (0,)))
    sig = 1.0 / (1.0 + jnp.exp(-gate_act))
    silu = gate_act * sig
    hidden = (silu * up_act).astype(bfloat)
    dhidden = dot32(d, down, ((1,), (1,)))
    gate_lin = (dhidden * up_act * sig * (1.0 + gate_act * (1.0 - sig))).astype(bfloat)
    up_lin = (dhidden * silu).astype(bfloat)
    return hidden, gate_lin, up_lin


def cut_of(array, ids_ref, near, far, span):
    parts = [
        array[:, pl.ds(pl.multiple_of((u * near + ids_ref[0]) * span, span), span)]
        for u in range(far)
    ]
    return parts[0] if far == 1 else jnp.concatenate(parts, axis=1)


def own_kernel(
    groups, block, cap, near, far, span, ids_ref, rank_ref, prob_ref, mid_even, mid_odd, cot_even,
    cot_odd, gate_ref, up_ref, down_ref, all_prob_ref, router_ref, hidden_out, gate_out, up_out,
    x_cut, d_cut, moe_even, moe_odd, dmid_even, dmid_odd, dlog_ref, rows_x, rows_d, sum_r, sum_x,
):
    e = pl.program_id(0)
    f = pl.program_id(1)

    @pl.when(f == 0)
    def _():
        def put(g, entered, dreturned):
            rows_x[g * cap : (g + 1) * cap, :] = entered
            rows_d[g * cap : (g + 1) * cap, :] = dreturned

        enter_rows(
            ids_ref, rank_ref, prob_ref, (mid_even, mid_odd), (cot_even, cot_odd), groups, block, cap, put
        )
        x_cut[0] = cut_of(rows_x, ids_ref, near, far, span)
        d_cut[0] = cut_of(rows_d, ids_ref, near, far, span)

    hidden, gate_lin, up_lin = hidden_and_gradients(
        rows_x[...], rows_d[...], gate_ref[0], up_ref[0], down_ref[0]
    )
    hidden_out[0] = hidden
    gate_out[0] = gate_lin
    up_out[0] = up_lin

    def parts():
        r_part = dot32(hidden, down_ref[0], ((1,), (0,)))
        x_part = dot32(gate_lin, gate_ref[0], ((1,), (1,))) + dot32(
            up_lin, up_ref[0], ((1,), (1,))
        )
        return r_part, x_part

    @pl.when(f == 0)
    def _():
        sum_r[...], sum_x[...] = parts()

    @pl.when(f > 0)
    def _():
        r_part, x_part = parts()
        sum_r[...] += r_part
        sum_x[...] += x_part

    @pl.when(f == pl.num_programs(1) - 1)
    def _():
        half = block // 2
        experts = all_prob_ref.shape[1]
        expert_row = lax.broadcasted_iota(jnp.int32, (experts, block), 0)
        spots = lax.broadcasted_iota(jnp.int32, (cap, block), 0).astype(single) + 1.0
        for g in range(groups):
            pick = rank_ref[0, 0, g : g + 1, :] == spots
            pick_f = pick.astype(single)
            pick_b = pick_f.astype(bfloat)
            weighted = (pick_f * prob_ref[0, 0, g : g + 1, :]).astype(bfloat)
            returned = sum_r[g * cap : (g + 1) * cap, :].astype(bfloat)
            cot_row = dot32(
                pick_b, rows_of_group((cot_even, cot_odd), g, groups), ((1,), (0,))
            )
            dgate = jnp.sum(cot_row * returned.astype(single), axis=1, keepdims=True)
            dgate = jnp.sum(jnp.where(pick, dgate, 0.0), axis=0, keepdims=True)
            probs = all_prob_ref[g]
            mine = jnp.where(expert_row == ids_ref[1] + e, dgate, 0.0)
            inner = jnp.sum(probs * mine, axis=0, keepdims=True)
            dlog = probs * (mine - inner)
            moe = dot32(weighted, returned, ((0,), (0,)))
            dmid = dot32(
                pick_b, sum_x[g * cap : (g + 1) * cap, :].astype(bfloat), ((0,), (0,))
            ) + dot32(dlog.astype(bfloat), router_ref[...], ((0,), (0,)))
            rows = slice(g * half, (g + 1) * half)

            @pl.when(e == 0)
            def _():
                dlog_ref[g] = dlog
                moe_even[rows, :] = moe[:half].astype(bfloat)
                moe_odd[rows, :] = moe[half:].astype(bfloat)
                dmid_even[rows, :] = dmid[:half].astype(bfloat)
                dmid_odd[rows, :] = dmid[half:].astype(bfloat)

            @pl.when(e > 0)
            def _():
                dlog_ref[g] += dlog
                for ref, add in (
                    (moe_even, moe[:half]),
                    (moe_odd, moe[half:]),
                    (dmid_even, dmid[:half]),
                    (dmid_odd, dmid[half:]),
                ):
                    ref[rows, :] = (ref[rows, :].astype(single) + add).astype(bfloat)


def others_kernel(
    mids, cots, groups, block, cap, near, far, span, more, ids_ref, rank_ref, prob_ref, *refs
):
    mid_refs, cot_refs, refs = refs[:mids], refs[mids : mids + cots], refs[mids + cots :]
    gate_ref, up_ref, down_ref = refs[:3]
    refs = refs[3:]
    if more:
        own_refs, in_refs, refs = refs[:5], refs[5:8], refs[8:]
    gate_out, up_out, down_out, rows_x, rows_d, hidden_all, gate_all, up_all = refs
    f = pl.program_id(1)
    p = pl.program_id(2)
    height = groups * cap

    @pl.when(f == 0)
    def _():
        def put(g, entered, dreturned):
            rows_x[pl.ds(p * height + g * cap, cap), :] = entered
            rows_d[pl.ds(p * height + g * cap, cap), :] = dreturned

        enter_rows(ids_ref, rank_ref, prob_ref, mid_refs, cot_refs, groups, block, cap, put)

    here = pl.ds(pl.multiple_of(p * height, 16), height)
    hidden, gate_lin, up_lin = hidden_and_gradients(
        rows_x[here, :], rows_d[here, :], gate_ref[0], up_ref[0], down_ref[0]
    )
    hidden_all[here, :] = hidden
    gate_all[here, :] = gate_lin
    up_all[here, :] = up_lin

    @pl.when(p == pl.num_programs(2) - 1)
    def _():
        x_cut = cut_of(rows_x, ids_ref, near, far, span)
        d_cut = cut_of(rows_d, ids_ref, near, far, span)
        gate_part = dot32(x_cut, gate_all[...], ((0,), (0,)))
        up_part = dot32(x_cut, up_all[...], ((0,), (0,)))
        down_part = dot32(hidden_all[...], d_cut, ((0,), (0,)))
        if more:
            x_own, d_own, hidden_own, gate_own, up_own = [ref[0] for ref in own_refs]
            gate_part += in_refs[0][0] + dot32(x_own, gate_own, ((0,), (0,)))
            up_part += in_refs[1][0] + dot32(x_own, up_own, ((0,), (0,)))
            down_part += in_refs[2][0] + dot32(hidden_own, d_own, ((0,), (0,)))
        gate_out[0] = gate_part
        up_out[0] = up_part
        down_out[0] = down_part


vmem = 60 * 1024 * 1024
chunk_units = 512


def routed_own(ids, cap, near, far, rank, prob, mid, cot, gate, up, down, probs, router_t):
    local, _, groups, block = rank.shape
    model = mid[0].shape[-1]
    tokens = groups * block
    units = gate.shape[2]
    chunk = min(chunk_units, units)
    span = model // (near * far)
    own_cols = far * span
    height = groups * cap

    def fixed(shape):
        return pl.BlockSpec(shape, lambda e, f, s: (0,) * len(shape), pipeline_mode=pl.Buffered(1))

    table = pl.BlockSpec((1, 1, groups, block), lambda e, f, s: (e, 0, 0, 0))
    wide = pl.BlockSpec((1, model, chunk), lambda e, f, s: (e, 0, f))
    tall = pl.BlockSpec((1, chunk, model), lambda e, f, s: (e, f, 0))
    lin = pl.BlockSpec((1, height, chunk), lambda e, f, s: (e, 0, f))
    cut = pl.BlockSpec((1, height, own_cols), lambda e, f, s: (e, 0, 0))
    args = [rank, prob, *mid, *cot, gate, up, down, probs, router_t]
    return pl.pallas_call(
        functools.partial(own_kernel, groups, block, cap, near, far, span),
        grid_spec=pltpu.PrefetchScalarGridSpec(
            num_scalar_prefetch=1,
            grid=(local, units // chunk),
            in_specs=[table, table]
            + [fixed(piece.shape) for piece in (*mid, *cot)]
            + [wide, wide, tall, fixed(probs.shape), fixed(router_t.shape)],
            out_specs=[lin] * 3 + [cut] * 2 + [fixed((tokens // 2, model))] * 4 + [fixed(probs.shape)],
            scratch_shapes=[pltpu.VMEM((height, model), bfloat)] * 2
            + [pltpu.VMEM((height, model), single)] * 2,
        ),
        out_shape=[jax.ShapeDtypeStruct((local, height, units), bfloat)] * 3
        + [jax.ShapeDtypeStruct((local, height, own_cols), bfloat)] * 2
        + [jax.ShapeDtypeStruct((tokens // 2, model), bfloat)] * 4
        + [jax.ShapeDtypeStruct(probs.shape, single)],
        compiler_params=pltpu.CompilerParams(
            dimension_semantics=("arbitrary",) * 2, vmem_limit_bytes=vmem
        ),
        cost_estimate=pl.CostEstimate(
            flops=12 * local * height * model * units,
            bytes_accessed=48 << 20,
            transcendentals=height * units,
        ),
        name="routed_own",
    )(ids, *args)


def routed_others(ids, cap, near, far, rank, prob, mid, cot, gate, up, down, more=None):
    local, planes, groups, block = rank.shape
    model = mid[0].shape[-1]
    units = gate.shape[2]
    chunk = min(chunk_units, units)
    span = model // (near * far)
    own_cols = far * span
    height = groups * cap
    mode = pl.Buffered(1) if planes == 1 else None

    def at_plane(ndim):
        def place(e, f, p, s):
            return (s[2 + jnp.where(f == 0, p, planes - 1)],) + (0,) * (ndim - 1)

        return place

    def rows_spec(piece):
        return pl.BlockSpec((1,) + piece.shape[1:], at_plane(piece.ndim), pipeline_mode=mode)

    table = pl.BlockSpec((1, 1, groups, block), lambda e, f, p, s: (e, p, 0, 0))
    wide = pl.BlockSpec((1, model, chunk), lambda e, f, p, s: (e, 0, f))
    tall = pl.BlockSpec((1, chunk, model), lambda e, f, p, s: (e, f, 0))
    wide_grad = pl.BlockSpec((1, own_cols, chunk), lambda e, f, p, s: (e, 0, f))
    tall_grad = pl.BlockSpec((1, chunk, own_cols), lambda e, f, p, s: (e, f, 0))
    lin = pl.BlockSpec((1, height, chunk), lambda e, f, p, s: (e, 0, f))
    cut = pl.BlockSpec((1, height, own_cols), lambda e, f, p, s: (e, 0, 0))
    in_specs = [table, table] + [rows_spec(piece) for piece in (*mid, *cot)] + [wide, wide, tall]
    args = [rank, prob, *mid, *cot, gate, up, down]
    aliases = {}
    if more is not None:
        in_specs += [cut, cut, lin, lin, lin, wide_grad, wide_grad, tall_grad]
        args += list(more)
        aliases = {len(args) - 2: 0, len(args) - 1: 1, len(args): 2}
    return pl.pallas_call(
        functools.partial(
            others_kernel, len(mid), len(cot), groups, block, cap, near, far, span, more is not None
        ),
        grid_spec=pltpu.PrefetchScalarGridSpec(
            num_scalar_prefetch=1,
            grid=(local, units // chunk, planes),
            in_specs=in_specs,
            out_specs=[wide_grad, wide_grad, tall_grad],
            scratch_shapes=[pltpu.VMEM((planes * height, model), bfloat)] * 2
            + [pltpu.VMEM((planes * height, chunk), bfloat)] * 3,
        ),
        out_shape=[
            jax.ShapeDtypeStruct((local, own_cols, units), single),
            jax.ShapeDtypeStruct((local, own_cols, units), single),
            jax.ShapeDtypeStruct((local, units, own_cols), single),
        ],
        input_output_aliases=aliases,
        compiler_params=pltpu.CompilerParams(
            dimension_semantics=("arbitrary",) * 3, vmem_limit_bytes=vmem
        ),
        cost_estimate=pl.CostEstimate(
            flops=8 * local * planes * height * model * units,
            bytes_accessed=64 << 20,
            transcendentals=planes * height * units,
        ),
        name="routed_others",
    )(ids, *args)


def masked_scores(scale, q, k, place_q, place_k, piece_q, piece_k):
    allowed = (place_k <= place_q) | ((piece_q == piece_k) & (piece_q > 0))
    return jnp.where(allowed, dot32(q, k, ((1,), (1,))) * scale, -1e30)


def attend_kernel(scale, q_ref, k_ref, v_ref, pq_ref, pk_ref, cq_ref, ck_ref, out_ref, mass_ref):
    scores = masked_scores(
        scale, q_ref[...], k_ref[...], pq_ref[...], pk_ref[...], cq_ref[...], ck_ref[...]
    )
    highest = jnp.max(scores, axis=-1, keepdims=True)
    exponent = jnp.exp(scores - highest)
    total = jnp.sum(exponent, axis=-1, keepdims=True)
    probs = (exponent / total).astype(bfloat)
    out_ref[...] = dot32(probs, v_ref[...], ((1,), (0,))).astype(bfloat)
    mass_ref[0] = highest + jnp.log(total)


def attend_back_kernel(
    scale, q_ref, k_ref, v_ref, da_ref, mass_ref, pq_ref, pk_ref, cq_ref, ck_ref, dq_ref, dk_ref, dv_ref
):
    q, k, v, da = q_ref[...], k_ref[...], v_ref[...], da_ref[...]
    scores = masked_scores(scale, q, k, pq_ref[...], pk_ref[...], cq_ref[...], ck_ref[...])
    probs = jnp.exp(scores - mass_ref[0])
    dprob = dot32(da, v, ((1,), (1,)))
    dsum = jnp.sum(probs * dprob, axis=-1, keepdims=True)
    dscores = (probs * (dprob - dsum)).astype(bfloat)
    dq_ref[...] = dot32(dscores, k, ((1,), (0,))) * scale
    dk = dot32(dscores, q, ((0,), (0,))) * scale
    dv = dot32(probs.astype(bfloat), da, ((0,), (0,)))

    @pl.when(pl.program_id(1) == 0)
    def _():
        dk_ref[...] = dk
        dv_ref[...] = dv

    @pl.when(pl.program_id(1) > 0)
    def _():
        dk_ref[...] += dk
        dv_ref[...] += dv


def attention_call(kernel, name, arrays, masses, marks, out_kinds, products):
    length, width = arrays[0][1].shape
    heads = width // HEAD
    span = min(256, length)
    by_query = pl.BlockSpec((span, HEAD), lambda h, i: (i, h))
    by_head = pl.BlockSpec((length, HEAD), lambda h, i: (0, h))
    mass = pl.BlockSpec((1, span, 1), lambda h, i: (h, i, 0))
    column = pl.BlockSpec((span, 1), lambda h, i: (i, 0))
    row = pl.BlockSpec((1, length), lambda h, i: (0, 0))
    specs = {"query": by_query, "head": by_head, "mass": mass}
    shapes = {"query": (length, width), "head": (length, width), "mass": (heads, length, 1)}
    mark_args = []
    for mark in marks:
        mark_args += [mark[:, None], mark[None, :]]
    return pl.pallas_call(
        kernel,
        grid=(heads, length // span),
        in_specs=[specs[kind] for kind, _ in arrays]
        + [mass] * len(masses)
        + [column, row] * len(marks),
        out_specs=[specs[kind] for kind, _ in out_kinds],
        out_shape=[jax.ShapeDtypeStruct(shapes[kind], dtype) for kind, dtype in out_kinds],
        compiler_params=pltpu.CompilerParams(
            dimension_semantics=("arbitrary",) * 2, vmem_limit_bytes=32 * 1024 * 1024
        ),
        cost_estimate=pl.CostEstimate(
            flops=2 * products * heads * length * length * HEAD,
            bytes_accessed=8 * length * width,
            transcendentals=heads * length * length,
        ),
        name=name,
    )(*[array for _, array in arrays], *masses, *mark_args)


def per_device(
    tokens,
    attn_query,
    attn_key,
    attn_value,
    attn_output,
    norm_in,
    norm_query,
    norm_key,
    norm_mid,
    router,
    expert_gate,
    expert_up,
    expert_down,
    routes,
    pieces,
    cotangent,
):
    n = lax.axis_size("expert")
    m = lax.axis_size("dp")
    rows, model = tokens.shape
    shard = attn_query.shape[0]
    experts = router.shape[1]
    top = routes.shape[1]
    local = expert_gate.shape[0]
    length = rows * n
    near = min(m, 4)
    far = m // near
    half = n // 2
    width = model // n
    heads = width // HEAD
    block = 2 * rows
    mine = lax.axis_index("expert")
    plane = lax.axis_index("dp")
    ready = routes[0, 0] >= 0
    scale = HEAD ** (-0.5)
    order = slot_order()
    slots = jnp.asarray(order, jnp.int32) ^ mine
    cap = -(-2 * min(rows, rows * top // experts + rows // 32) // 16) * 16

    parts = jnp.stack([attn_query, attn_key, attn_value]).reshape(3, shard, n, width)
    parts_out = parts.transpose(2, 0, 1, 3)
    parts = lax.all_to_all(parts_out, "expert", split_axis=0, concat_axis=0, tiled=True)
    parts = parts.transpose(1, 0, 2, 3).reshape(3, n * shard, width)

    def all_rows(part, first=None):
        held, places = gather_steps(part, "dp", m, first)
        out = []
        for kind in range(part.shape[0]):
            full = jnp.zeros((m, n * shard, width), bfloat)
            for at, kd in enumerate(places):
                full = lax.dynamic_update_slice(
                    full, held[at, kind][None], (plane ^ kd, jnp.int32(0), jnp.int32(0))
                )
            out.append(full.reshape(model, width))
        return out

    packed = jnp.concatenate(
        [norm_in[None], norm_query[None], norm_key[None], norm_mid[None], router.T], axis=0
    )
    kinds = packed.shape[0]
    packed = jnp.concatenate(
        [
            jnp.pad(packed.reshape(-1), (0, -kinds * shard % HEAD)).reshape(-1, HEAD),
            routes.T.astype(bfloat).reshape(top * rows // HEAD, HEAD),
            pieces.astype(bfloat).reshape(rows // HEAD, HEAD),
        ],
        axis=0,
    )
    packed = after(packed, parts_out)
    small, places = gather_steps(packed, "dp", m)
    first_rows = swap(after(parts[None], small), "dp", m - 1)
    small = jnp.stack([small[places.index(kd)] for kd in range(m)])
    small = jnp.concatenate(gather_halves(small), axis=0)
    chips = gather_chips(after(jnp.stack([tokens, cotangent]), parts))
    x_even = after(jnp.stack([piece[0] for piece in chips]), first_rows)
    x_odd = swap(x_even, "expert", 1)
    cot_even = jnp.stack([piece[1] for piece in chips])
    cot_odd = swap(cot_even, "expert", 1)
    w_q, w_k, w_v = all_rows(parts, first_rows)
    cut = -(-kinds * shard // HEAD)
    gains = jnp.take(small[:, :, :cut], jnp.asarray([order.index(j) for j in range(n)]), axis=0)
    gains = jnp.take(gains, jnp.arange(n, dtype=jnp.int32) ^ mine, axis=0)
    gains = jnp.take(gains, jnp.arange(m, dtype=jnp.int32) ^ plane, axis=1)
    gains = gains.reshape(n, m, -1)[:, :, : kinds * shard].reshape(n, m, kinds, shard).transpose(2, 1, 0, 3).reshape(kinds, model)
    gain_in, gain_query, gain_key, gain_mid = [gains[i].astype(single) for i in range(4)]
    router_t = gains[4:]
    piece_row = small[:, 0, cut + top * rows // HEAD :].reshape(length)
    route_rows = small[:, :, cut : cut + top * rows // HEAD].reshape(n, m, top, rows)

    x = jnp.concatenate([x_even, x_odd], axis=0).reshape(length, model).astype(single)
    rs_in = lax.rsqrt(jnp.mean(x * x, axis=-1, keepdims=True) + eps_norm)
    normed_b = (x * rs_in * gain_in).astype(bfloat)

    near_groups = [[g * near + i for i in range(near)] for g in range(far)] if far > 1 else None
    cot_planes = lax.all_gather(after(cot_even, w_v), "dp", axis=0, axis_index_groups=near_groups)

    place = (slots[:, None] * rows + jnp.arange(rows, dtype=jnp.int32)[None, :]).reshape(length)
    turn_half = HEAD // 2
    inverse = jnp.exp(jnp.arange(turn_half, dtype=single) * (-2.0 * math.log(rope_base) / HEAD))
    angles = place.astype(single)[:, None] * inverse[None, :]
    cosine = jnp.cos(angles)
    sine = jnp.sin(angles)

    def rotate(values, back):
        out = []
        sn = -sine if back else sine
        for h in range(heads):
            u = values[:, h * HEAD : h * HEAD + turn_half]
            w = values[:, h * HEAD + turn_half : (h + 1) * HEAD]
            out += [u * cosine - w * sn, w * cosine + u * sn]
        return jnp.concatenate(out, axis=-1)

    own_gain_q = lax.dynamic_slice_in_dim(gain_query, mine * width, width)
    own_gain_k = lax.dynamic_slice_in_dim(gain_key, mine * width, width)
    def halves(array):
        return array[: length // 2], array[length // 2 :]

    upper = (
        jnp.arange(block, dtype=jnp.int32)[:, None] <= jnp.arange(block, dtype=jnp.int32)[None, :]
    ).astype(bfloat)
    ids = (mine * local + jnp.arange(local, dtype=jnp.int32)).astype(bfloat)

    def ranks(kd):
        named = route_rows[:, kd]
        hit = jnp.any(named[None] == ids[:, None, None, None], axis=2)
        hit = jnp.concatenate([hit[:, :half], hit[:, half:]], axis=-1)
        rank = lax.dot_general(
            hit.astype(bfloat), upper, (((2,), (0,)), ((), ())), preferred_element_type=single
        )
        return jnp.where(hit, rank, 0.0)

    own_ranks = after(ranks(0)[:, None], cot_odd)

    x_own = tokens.astype(single)

    marks = [place, piece_row.astype(jnp.int32)]

    def forward():
        query_raw = dot32(normed_b, w_q, ((1,), (0,)))
        key_raw = dot32(normed_b, w_k, ((1,), (0,)))
        own_shards = []
        send = attn_output
        for turn in range(m):
            pairs = [(s, ((s % m + turn) % m) * n + s // m) for s in range(m * n)]
            own_shards.append(lax.ppermute(send, ("dp", "expert"), pairs))
        wo = jnp.zeros((m, shard, model), bfloat)
        for turn in range(m):
            wo = lax.dynamic_update_slice(
                wo, own_shards[turn][None], ((plane - turn) % m, jnp.int32(0), jnp.int32(0))
            )
        wo = wo.reshape(width, model)

        squares = jnp.stack([jnp.sum(query_raw**2, axis=-1), jnp.sum(key_raw**2, axis=-1)])
        squares = sum_rows_over_expert(squares.reshape(2, n, rows)).reshape(2, length)
        rs_q = lax.rsqrt(squares[0] / model + eps_norm)[:, None]
        rs_k = lax.rsqrt(squares[1] / model + eps_norm)[:, None]
        value_b = dot32(normed_b, w_v, ((1,), (0,))).astype(bfloat)

        query_b = rotate(query_raw * rs_q * own_gain_q, False).astype(bfloat)
        key_b = rotate(key_raw * rs_k * own_gain_k, False).astype(bfloat)

        attended, masses = attention_call(
            functools.partial(attend_kernel, scale),
            "attend",
            [("query", query_b), ("head", key_b), ("head", value_b)],
            [],
            marks,
            [("query", bfloat), ("mass", single)],
            2,
        )

        projected = [dot32(part, wo, ((1,), (0,))).astype(bfloat) for part in halves(attended)]
        residual = x_own + scatter_sum(*projected)
        rs_mid = lax.rsqrt(jnp.mean(residual * residual, axis=-1, keepdims=True) + eps_norm)
        mid = after(residual * rs_mid * gain_mid, own_ranks).astype(bfloat)
        mid_even, mid_odd = gather_halves(mid)
        kept = (query_raw, key_raw, rs_q, rs_k, query_b, key_b, value_b, wo)
        return kept, masses, attended, residual, rs_mid, mid_even, mid_odd

    kept, masses, attended, residual, rs_mid, mid_even, mid_odd = stage(ready, forward)
    query_raw, key_raw, rs_q, rs_k, query_b, key_b, value_b, wo = kept
    mid_planes = lax.all_gather(after(mid_even, cot_planes), "dp", axis=0, axis_index_groups=near_groups)

    def router_probs_of(mid_rows):
        logits = dot32(router_t, mid_rows.reshape(-1, model), ((1,), (1,)))
        exponent = jnp.exp(logits - jnp.max(logits, axis=0, keepdims=True))
        return exponent / jnp.sum(exponent, axis=0, keepdims=True)

    def local_probs(array):
        return lax.dynamic_slice_in_dim(array, mine * local, local, 0)

    def grouped(even, odd):
        return jnp.concatenate(
            [even.reshape(-1, half, rows), odd.reshape(-1, half, rows)], axis=-1
        )

    router_probs = grouped(router_probs_of(mid_even), router_probs_of(mid_odd))
    fixed_ids = jnp.stack([plane % near, mine * local])

    def by_group(blocks):
        return jnp.stack([blocks[:half], blocks[half:]], axis=1).reshape(n)

    def backward():
        own_out = routed_own(
            fixed_ids,
            cap,
            near,
            far,
            own_ranks,
            local_probs(router_probs)[:, None],
            [mid_even[None], mid_odd[None]],
            [cot_even[None], cot_odd[None]],
            expert_gate,
            expert_up,
            expert_down,
            router_probs.transpose(1, 0, 2),
            router_t,
        )
        hidden_own, gate_lin_own, up_lin_own, x_own_cut, d_own_cut = own_out[:5]
        moe_even, moe_odd, dmid_even, dmid_odd, dlogits = own_out[5:]
        dmid = scatter_sum(dmid_even, dmid_odd)
        scaled = dmid * gain_mid
        mid_grad = jnp.sum(dmid * (residual * rs_mid), axis=0)
        inner = jnp.mean(scaled * residual, axis=-1, keepdims=True)
        dres = cotangent.astype(single) + rs_mid * (scaled - residual * (rs_mid * rs_mid * inner))
        dres_chips = gather_chips(dres.astype(bfloat))
        dres_even = jnp.stack(dres_chips)
        dres_odd = swap(dres_even, "expert", 1).reshape(-1, model)
        dres_even = dres_even.reshape(-1, model)
        datt_b = jnp.concatenate(
            [dot32(part, wo, ((1,), (1,))) for part in (dres_even, dres_odd)], axis=0
        )
        datt_b = datt_b.astype(bfloat)

        moe_pairs = pair_sums(after(moe_even, dres_odd), after(moe_odd, dres_odd))
        cot_planes_odd = swap(cot_planes, "expert", 1)
        gate_tables = [swap(local_probs(router_probs), "dp", kd) for kd in range(1, near)]

        dq_rot, dk_rot, dv = attention_call(
            functools.partial(attend_back_kernel, scale),
            "attend_back",
            [("query", query_b), ("head", key_b), ("head", value_b), ("query", datt_b)],
            [masses],
            marks,
            [("query", single), ("head", single), ("head", single)],
            5,
        )
        dq_un = rotate(dq_rot, True)
        dk_un = rotate(dk_rot, True)
        inners = jnp.stack(
            [
                jnp.sum(dq_un * own_gain_q * query_raw, axis=-1),
                jnp.sum(dk_un * own_gain_k * key_raw, axis=-1),
            ]
        )
        inners = sum_rows_over_expert(inners.reshape(2, n, rows)).reshape(2, length)
        query_gain_grad = jnp.sum(dq_un * query_raw * rs_q, axis=0)
        key_gain_grad = jnp.sum(dk_un * key_raw * rs_k, axis=0)
        dq_b = (
            rs_q * dq_un * own_gain_q - query_raw * (rs_q**3 / model * inners[0][:, None])
        ).astype(bfloat)
        dk_b = (
            rs_k * dk_un * own_gain_k - key_raw * (rs_k**3 / model * inners[1][:, None])
        ).astype(bfloat)
        dv_b = dv.astype(bfloat)
        dnormed_part = [
                (
                    dot32(dq_part, w_q, ((1,), (1,)))
                    + dot32(dk_part, w_k, ((1,), (1,)))
                    + dot32(dv_part, w_v, ((1,), (1,)))
                ).astype(bfloat)
                for dq_part, dk_part, dv_part in zip(halves(dq_b), halves(dk_b), halves(dv_b))
        ]
        output_part = dot32(dres_even, attended[: length // 2], ((0,), (0,))) + dot32(
            dres_odd, attended[length // 2 :], ((0,), (0,))
        )
        early = jnp.stack([dot32(normed_b, dv_b, ((0,), (0,))), output_part]).astype(bfloat)
        late = jnp.stack([dot32(normed_b, part, ((0,), (0,))) for part in (dq_b, dk_b)])
        late = late.astype(bfloat)
        return (
            own_out,
            dres,
            dres_even,
            dres_odd,
            mid_grad,
            query_gain_grad,
            key_gain_grad,
            dq_b,
            dk_b,
            dv_b,
            dnormed_part,
            moe_pairs,
            cot_planes_odd,
            gate_tables,
            early,
            late,
        )

    (
        own_out,
        dres,
        dres_even,
        dres_odd,
        mid_grad,
        query_gain_grad,
        key_gain_grad,
        dq_b,
        dk_b,
        dv_b,
        dnormed_part,
        moe_pairs,
        cot_planes_odd,
        gate_tables,
        early,
        late,
    ) = stage(ready, backward)
    hidden_own, gate_lin_own, up_lin_own, x_own_cut, d_own_cut = own_out[:5]
    moe_even, moe_odd, dmid_even, dmid_odd, dlogits = own_out[5:]
    dnormed = scatter_sum(*dnormed_part)
    dnormed_part = dnormed_part[0]

    dlogits = dlogits.transpose(1, 0, 2).astype(bfloat)
    router_grad = dot32(
        dlogits[:, :, :rows].reshape(experts, -1), mid_even.reshape(-1, model), ((1,), (0,))
    ) + dot32(dlogits[:, :, rows:].reshape(experts, -1), mid_odd.reshape(-1, model), ((1,), (0,)))

    mid_planes = [mid_planes, swap(mid_planes, "expert", 1)]
    cot_planes = [cot_planes, cot_planes_odd]
    def add_sequences(masks, more, *earlier):
        planes = [plane % near ^ kd for kd in masks]
        return routed_others(
            jnp.concatenate([plane[None] % near, jnp.full((1,), len(masks), jnp.int32), jnp.stack(planes)]),
            cap,
            near,
            far,
            after(jnp.stack([ranks(kd) for kd in masks], axis=1), *earlier),
            jnp.stack([gate_tables[kd - 1] for kd in masks], axis=1),
            mid_planes,
            cot_planes,
            expert_gate,
            expert_up,
            expert_down,
            more,
        )

    late = lax.psum_scatter(late, "dp", scatter_dimension=1, tiled=True)
    early = lax.psum_scatter(early, "dp", scatter_dimension=1, tiled=True)
    moe = sum_chips(moe_pairs)
    weight_sums = add_sequences(list(range(1, near - 1)), None, dnormed_part)
    dnormed = after(dnormed, weight_sums[0])
    summed = jnp.concatenate([early[:1], late], axis=0)
    moved = lax.all_to_all(
        after(summed, weight_sums[0]).reshape(3, n, shard, width).transpose(1, 0, 2, 3),
        "expert",
        split_axis=0,
        concat_axis=0,
        tiled=True,
    )
    moved = moved.transpose(1, 2, 0, 3).reshape(3, shard, model).astype(single)
    value_grad, query_grad, key_grad = moved[0], moved[1], moved[2]
    output_sum = after(early[1], weight_sums[0]).reshape(model // m, m, shard).transpose(1, 2, 0)
    pieces_here = []
    for turn in range(m):
        pairs = [(((s % m + turn) % m) * n + s // m, s) for s in range(m * n)]
        sent = lax.dynamic_index_in_dim(output_sum, (plane - turn) % m, 0, keepdims=False)
        pieces_here.append(lax.ppermute(sent, ("dp", "expert"), pairs))
    shard_at = (plane * n + mine) % m
    output_grad = jnp.take(
        jnp.stack(pieces_here), (jnp.arange(m, dtype=jnp.int32) - shard_at) % m, axis=0
    )
    output_grad = output_grad.transpose(1, 0, 2).reshape(shard, model).astype(single)

    output = (residual + moe).astype(bfloat)
    rs_own = rs_in[:rows]
    scaled_in = dnormed * gain_in
    inner_in = jnp.mean(scaled_in * x_own, axis=-1, keepdims=True)
    input_grad = dres + rs_own * (scaled_in - x_own * (rs_own * rs_own * inner_in))
    in_grad = jnp.sum(dnormed * x_own * rs_own, axis=0)

    def placed(part):
        return lax.dynamic_update_slice(jnp.zeros((model,), single), part, (mine * width,))

    small_grad = jnp.concatenate(
        [
            in_grad[None],
            placed(query_gain_grad)[None],
            placed(key_gain_grad)[None],
            mid_grad[None],
            router_grad,
        ],
        axis=0,
    ).reshape(kinds, m, n, shard)
    small_grad = jnp.take(small_grad, jnp.arange(n, dtype=jnp.int32) ^ mine, axis=2)
    small_pair = small_grad[:, :, 0::2] + swap(small_grad[:, :, 1::2], "expert", 1)
    small_sum = small_pair[:, :, 0]
    for k in range(2, n, 2):
        small_sum = small_sum + swap(small_pair[:, :, k // 2], "expert", k)
    small_sum = jnp.take(small_sum, jnp.arange(m, dtype=jnp.int32) ^ plane, axis=1)
    total = small_sum[:, 0]
    for k in range(1, m):
        total = total + swap(small_sum[:, k], "dp", k)

    own_rows = [x_own_cut, d_own_cut, hidden_own, gate_lin_own, up_lin_own]
    weight_sums = add_sequences([near - 1], own_rows + list(weight_sums), moe)
    gate_grad, up_grad, down_grad = weight_sums
    span = model // m

    def sum_over_far(parts):
        if far == 1:
            return parts[0]
        parts = jnp.take(parts, jnp.arange(far, dtype=jnp.int32) ^ (plane // near), axis=0)
        total = parts[0]
        for k in range(1, far):
            total = total + swap(parts[k].astype(bfloat), "dp", k * near).astype(single)
        return total

    units = expert_gate.shape[2]
    gate_grad, up_grad = [
        sum_over_far(grad.reshape(local, far, span, units).transpose(1, 0, 2, 3))
        for grad in (gate_grad, up_grad)
    ]
    down_grad = sum_over_far(down_grad.reshape(local, units, far, span).transpose(2, 0, 1, 3))

    return (
        output,
        input_grad,
        query_grad,
        key_grad,
        value_grad,
        output_grad,
        total[0],
        total[1],
        total[2],
        total[3],
        total[4:].T,
        gate_grad,
        up_grad,
        down_grad,
    )


def solution(mesh):
    both = ("dp", "expert")
    in_specs = (
        [P(both, None)] * 5
        + [P(both)] * 4
        + [P(both, None)]
        + [P("expert", None, None)] * 3
        + [P(both, None), P(both), P(both, None)]
    )
    out_specs = (
        [P(both, None)] * 6
        + [P(both)] * 4
        + [P(both, None)]
        + [P("expert", "dp", None)] * 2
        + [P("expert", None, "dp")]
    )
    return jax.shard_map(
        per_device,
        mesh=mesh,
        in_specs=tuple(in_specs),
        out_specs=tuple(out_specs),
        check_vma=False,
    )
```

```python
import functools
import math

import jax
import jax.numpy as jnp
from jax import lax
from jax.experimental import pallas as pl
from jax.experimental.pallas import tpu as pltpu
from jax.sharding import PartitionSpec as P

HEAD = 128
eps_norm = 1e-05
rope_base = 10000.0
single = jnp.float32
bfloat = jnp.bfloat16


def dot32(left, right, dims):
    return lax.dot_general(left, right, (dims, ((), ())), preferred_element_type=single)


def after(values, *earlier):
    for result in earlier:
        zero = jnp.minimum(jnp.abs(result[(-1,) * result.ndim]), 0)
        values = values + zero.astype(values.dtype)
    return values


def swap(values, axis, mask):
    count = lax.axis_size(axis)
    return lax.ppermute(values, axis, [(i, i ^ mask) for i in range(count)])


def stage(ready, compute):
    shapes = jax.eval_shape(compute)
    return lax.cond(
        ready, compute, lambda: jax.tree.map(lambda a: jnp.zeros(a.shape, a.dtype), shapes)
    )


def slot_order():
    count = lax.axis_size("expert")
    return list(range(0, count, 2)) + list(range(1, count, 2))


def gather_chips(values):
    count = lax.axis_size("expert")
    return [values if mask == 0 else swap(values, "expert", mask) for mask in range(0, count, 2)]


def gather_halves(values, *earlier):
    even = after(jnp.stack(gather_chips(values)), *earlier)
    return even, swap(even, "expert", 1)


def gather_steps(values, axis, count, first=None):
    held = values[None]
    order = [0]
    mask = count - 1
    while mask > 0:
        other = first if first is not None and mask == count - 1 else swap(held, axis, mask)
        held = jnp.concatenate([held, other], axis=0)
        order = order + [place ^ mask for place in order]
        mask >>= 1
    return held, order


def pair_sums(even, odd):
    half = lax.axis_size("expert") // 2
    rows = even.shape[0] // half
    arrived = swap(odd, "expert", 1)
    parts = [slice(place * rows, (place + 1) * rows) for place in range(half)]
    return [(even[part].astype(single) + arrived[part].astype(single)).astype(bfloat) for part in parts]


def sum_chips(pairs):
    total = pairs[0].astype(single)
    for place in range(1, len(pairs)):
        total = total + swap(pairs[place], "expert", 2 * place).astype(single)
    return total


def scatter_sum(even, odd, with_first=False):
    half = lax.axis_size("expert") // 2
    rows = even.shape[0] // half
    arrived = swap(odd, "expert", 1)
    total = None
    for place in reversed(range(half)):
        part = slice(place * rows, (place + 1) * rows)
        pair = even[part].astype(single) + arrived[part].astype(single)
        if place > 0:
            pair = swap(pair.astype(bfloat), "expert", 2 * place).astype(single)
        if place == half - 1:
            first = arrived
        total = pair if total is None else total + pair
    return (total, first) if with_first else total


def sum_rows_over_expert(values):
    order = slot_order()

    def reorder(array, mask):
        return jnp.concatenate(
            [array[:, order.index(s ^ mask)][:, None] for s in order], axis=1
        )

    total = values + reorder(swap(values, "expert", 1), 1)
    out = total
    for mask in range(2, len(order), 2):
        out = out + reorder(swap(total, "expert", mask), mask)
    return out


def rows_of_group(pieces, g, groups):
    first = len(pieces) // 2
    share = groups // first
    at, part = g // share, g % share
    return jnp.concatenate([pieces[at][0, part], pieces[first + at][0, part]], axis=0)


def enter_rows(ids_ref, rank_ref, prob_ref, mid_refs, cot_refs, groups, block, cap, put):
    spots = lax.broadcasted_iota(jnp.int32, (cap, block), 0).astype(single) + 1.0
    for g in range(groups):
        pick = rank_ref[0, 0, g : g + 1, :] == spots
        pick_b = pick.astype(single).astype(bfloat)
        gate_col = jnp.sum(
            jnp.where(pick, prob_ref[0, 0, g : g + 1, :], 0.0), axis=1, keepdims=True
        )
        entered = dot32(pick_b, rows_of_group(mid_refs, g, groups), ((1,), (0,)))
        cot_row = dot32(pick_b, rows_of_group(cot_refs, g, groups), ((1,), (0,)))
        put(g, entered.astype(bfloat), (cot_row * gate_col).astype(bfloat))


def hidden_and_gradients(x, d, gate, up, down):
    gate_act = dot32(x, gate, ((1,), (0,)))
    up_act = dot32(x, up, ((1,), (0,)))
    sig = 1.0 / (1.0 + jnp.exp(-gate_act))
    silu = gate_act * sig
    hidden = (silu * up_act).astype(bfloat)
    dhidden = dot32(d, down, ((1,), (1,)))
    gate_lin = (dhidden * up_act * sig * (1.0 + gate_act * (1.0 - sig))).astype(bfloat)
    up_lin = (dhidden * silu).astype(bfloat)
    return hidden, gate_lin, up_lin


def cut_of(array, ids_ref, near, far, span):
    parts = [
        array[:, pl.ds(pl.multiple_of((u * near + ids_ref[0]) * span, span), span)]
        for u in range(far)
    ]
    return parts[0] if far == 1 else jnp.concatenate(parts, axis=1)


def own_kernel(
    groups, block, cap, near, far, span, ids_ref, rank_ref, prob_ref, mid_even, mid_odd, cot_even,
    cot_odd, gate_ref, up_ref, down_ref, all_prob_ref, router_ref, hidden_out, gate_out, up_out,
    x_cut, d_cut, moe_even, moe_odd, dmid_even, dmid_odd, dlog_ref, rows_x, rows_d, sum_r, sum_x,
):
    e = pl.program_id(0)
    f = pl.program_id(1)

    @pl.when(f == 0)
    def _():
        def put(g, entered, dreturned):
            rows_x[g * cap : (g + 1) * cap, :] = entered
            rows_d[g * cap : (g + 1) * cap, :] = dreturned

        enter_rows(
            ids_ref, rank_ref, prob_ref, (mid_even, mid_odd), (cot_even, cot_odd), groups, block, cap, put
        )
        x_cut[0] = cut_of(rows_x, ids_ref, near, far, span)
        d_cut[0] = cut_of(rows_d, ids_ref, near, far, span)

    hidden, gate_lin, up_lin = hidden_and_gradients(
        rows_x[...], rows_d[...], gate_ref[0], up_ref[0], down_ref[0]
    )
    hidden_out[0] = hidden
    gate_out[0] = gate_lin
    up_out[0] = up_lin

    def parts():
        r_part = dot32(hidden, down_ref[0], ((1,), (0,)))
        x_part = dot32(gate_lin, gate_ref[0], ((1,), (1,))) + dot32(
            up_lin, up_ref[0], ((1,), (1,))
        )
        return r_part, x_part

    @pl.when(f == 0)
    def _():
        sum_r[...], sum_x[...] = parts()

    @pl.when(f > 0)
    def _():
        r_part, x_part = parts()
        sum_r[...] += r_part
        sum_x[...] += x_part

    @pl.when(f == pl.num_programs(1) - 1)
    def _():
        half = block // 2
        experts = all_prob_ref.shape[1]
        expert_row = lax.broadcasted_iota(jnp.int32, (experts, block), 0)
        spots = lax.broadcasted_iota(jnp.int32, (cap, block), 0).astype(single) + 1.0
        for g in range(groups):
            pick = rank_ref[0, 0, g : g + 1, :] == spots
            pick_f = pick.astype(single)
            pick_b = pick_f.astype(bfloat)
            weighted = (pick_f * prob_ref[0, 0, g : g + 1, :]).astype(bfloat)
            returned = sum_r[g * cap : (g + 1) * cap, :].astype(bfloat)
            cot_row = dot32(
                pick_b, rows_of_group((cot_even, cot_odd), g, groups), ((1,), (0,))
            )
            dgate = jnp.sum(cot_row * returned.astype(single), axis=1, keepdims=True)
            dgate = jnp.sum(jnp.where(pick, dgate, 0.0), axis=0, keepdims=True)
            probs = all_prob_ref[g]
            mine = jnp.where(expert_row == ids_ref[1] + e, dgate, 0.0)
            inner = jnp.sum(probs * mine, axis=0, keepdims=True)
            dlog = probs * (mine - inner)
            moe = dot32(weighted, returned, ((0,), (0,)))
            dmid = dot32(
                pick_b, sum_x[g * cap : (g + 1) * cap, :].astype(bfloat), ((0,), (0,))
            ) + dot32(dlog.astype(bfloat), router_ref[...], ((0,), (0,)))
            rows = slice(g * half, (g + 1) * half)

            @pl.when(e == 0)
            def _():
                dlog_ref[g] = dlog
                moe_even[rows, :] = moe[:half].astype(bfloat)
                moe_odd[rows, :] = moe[half:].astype(bfloat)
                dmid_even[rows, :] = dmid[:half].astype(bfloat)
                dmid_odd[rows, :] = dmid[half:].astype(bfloat)

            @pl.when(e > 0)
            def _():
                dlog_ref[g] += dlog
                for ref, add in (
                    (moe_even, moe[:half]),
                    (moe_odd, moe[half:]),
                    (dmid_even, dmid[:half]),
                    (dmid_odd, dmid[half:]),
                ):
                    ref[rows, :] = (ref[rows, :].astype(single) + add).astype(bfloat)


def others_kernel(
    mids, cots, groups, block, cap, near, far, span, more, ids_ref, rank_ref, prob_ref, *refs
):
    mid_refs, cot_refs, refs = refs[:mids], refs[mids : mids + cots], refs[mids + cots :]
    gate_ref, up_ref, down_ref = refs[:3]
    refs = refs[3:]
    if more:
        own_refs, in_refs, refs = refs[:5], refs[5:8], refs[8:]
    gate_out, up_out, down_out, rows_x, rows_d, hidden_all, gate_all, up_all = refs
    f = pl.program_id(1)
    p = pl.program_id(2)
    height = groups * cap

    @pl.when(f == 0)
    def _():
        def put(g, entered, dreturned):
            rows_x[pl.ds(p * height + g * cap, cap), :] = entered
            rows_d[pl.ds(p * height + g * cap, cap), :] = dreturned

        enter_rows(ids_ref, rank_ref, prob_ref, mid_refs, cot_refs, groups, block, cap, put)

    here = pl.ds(pl.multiple_of(p * height, 16), height)
    hidden, gate_lin, up_lin = hidden_and_gradients(
        rows_x[here, :], rows_d[here, :], gate_ref[0], up_ref[0], down_ref[0]
    )
    hidden_all[here, :] = hidden
    gate_all[here, :] = gate_lin
    up_all[here, :] = up_lin

    @pl.when(p == pl.num_programs(2) - 1)
    def _():
        x_cut = cut_of(rows_x, ids_ref, near, far, span)
        d_cut = cut_of(rows_d, ids_ref, near, far, span)
        gate_part = dot32(x_cut, gate_all[...], ((0,), (0,)))
        up_part = dot32(x_cut, up_all[...], ((0,), (0,)))
        down_part = dot32(hidden_all[...], d_cut, ((0,), (0,)))
        if more:
            x_own, d_own, hidden_own, gate_own, up_own = [ref[0] for ref in own_refs]
            gate_part += in_refs[0][0] + dot32(x_own, gate_own, ((0,), (0,)))
            up_part += in_refs[1][0] + dot32(x_own, up_own, ((0,), (0,)))
            down_part += in_refs[2][0] + dot32(hidden_own, d_own, ((0,), (0,)))
        gate_out[0] = gate_part
        up_out[0] = up_part
        down_out[0] = down_part


vmem = 60 * 1024 * 1024
chunk_units = 512


def routed_own(ids, cap, near, far, rank, prob, mid, cot, gate, up, down, probs, router_t):
    local, _, groups, block = rank.shape
    model = mid[0].shape[-1]
    tokens = groups * block
    units = gate.shape[2]
    chunk = min(chunk_units, units)
    span = model // (near * far)
    own_cols = far * span
    height = groups * cap

    def fixed(shape):
        return pl.BlockSpec(shape, lambda e, f, s: (0,) * len(shape), pipeline_mode=pl.Buffered(1))

    table = pl.BlockSpec((1, 1, groups, block), lambda e, f, s: (e, 0, 0, 0))
    wide = pl.BlockSpec((1, model, chunk), lambda e, f, s: (e, 0, f))
    tall = pl.BlockSpec((1, chunk, model), lambda e, f, s: (e, f, 0))
    lin = pl.BlockSpec((1, height, chunk), lambda e, f, s: (e, 0, f))
    cut = pl.BlockSpec((1, height, own_cols), lambda e, f, s: (e, 0, 0))
    args = [rank, prob, *mid, *cot, gate, up, down, probs, router_t]
    return pl.pallas_call(
        functools.partial(own_kernel, groups, block, cap, near, far, span),
        grid_spec=pltpu.PrefetchScalarGridSpec(
            num_scalar_prefetch=1,
            grid=(local, units // chunk),
            in_specs=[table, table]
            + [fixed(piece.shape) for piece in (*mid, *cot)]
            + [wide, wide, tall, fixed(probs.shape), fixed(router_t.shape)],
            out_specs=[lin] * 3 + [cut] * 2 + [fixed((tokens // 2, model))] * 4 + [fixed(probs.shape)],
            scratch_shapes=[pltpu.VMEM((height, model), bfloat)] * 2
            + [pltpu.VMEM((height, model), single)] * 2,
        ),
        out_shape=[jax.ShapeDtypeStruct((local, height, units), bfloat)] * 3
        + [jax.ShapeDtypeStruct((local, height, own_cols), bfloat)] * 2
        + [jax.ShapeDtypeStruct((tokens // 2, model), bfloat)] * 4
        + [jax.ShapeDtypeStruct(probs.shape, single)],
        compiler_params=pltpu.CompilerParams(
            dimension_semantics=("arbitrary",) * 2, vmem_limit_bytes=vmem
        ),
        cost_estimate=pl.CostEstimate(
            flops=12 * local * height * model * units,
            bytes_accessed=48 << 20,
            transcendentals=height * units,
        ),
        name="routed_own",
    )(ids, *args)


def routed_others(ids, cap, near, far, rank, prob, mid, cot, gate, up, down, more=None):
    local, planes, groups, block = rank.shape
    model = mid[0].shape[-1]
    units = gate.shape[2]
    chunk = min(chunk_units, units)
    span = model // (near * far)
    own_cols = far * span
    height = groups * cap
    mode = pl.Buffered(1) if planes == 1 else None

    def at_plane(ndim):
        def place(e, f, p, s):
            return (s[2 + jnp.where(f == 0, p, planes - 1)],) + (0,) * (ndim - 1)

        return place

    def rows_spec(piece):
        return pl.BlockSpec((1,) + piece.shape[1:], at_plane(piece.ndim), pipeline_mode=mode)

    table = pl.BlockSpec((1, 1, groups, block), lambda e, f, p, s: (e, p, 0, 0))
    wide = pl.BlockSpec((1, model, chunk), lambda e, f, p, s: (e, 0, f))
    tall = pl.BlockSpec((1, chunk, model), lambda e, f, p, s: (e, f, 0))
    wide_grad = pl.BlockSpec((1, own_cols, chunk), lambda e, f, p, s: (e, 0, f))
    tall_grad = pl.BlockSpec((1, chunk, own_cols), lambda e, f, p, s: (e, f, 0))
    lin = pl.BlockSpec((1, height, chunk), lambda e, f, p, s: (e, 0, f))
    cut = pl.BlockSpec((1, height, own_cols), lambda e, f, p, s: (e, 0, 0))
    in_specs = [table, table] + [rows_spec(piece) for piece in (*mid, *cot)] + [wide, wide, tall]
    args = [rank, prob, *mid, *cot, gate, up, down]
    aliases = {}
    if more is not None:
        in_specs += [cut, cut, lin, lin, lin, wide_grad, wide_grad, tall_grad]
        args += list(more)
        aliases = {len(args) - 2: 0, len(args) - 1: 1, len(args): 2}
    return pl.pallas_call(
        functools.partial(
            others_kernel, len(mid), len(cot), groups, block, cap, near, far, span, more is not None
        ),
        grid_spec=pltpu.PrefetchScalarGridSpec(
            num_scalar_prefetch=1,
            grid=(local, units // chunk, planes),
            in_specs=in_specs,
            out_specs=[wide_grad, wide_grad, tall_grad],
            scratch_shapes=[pltpu.VMEM((planes * height, model), bfloat)] * 2
            + [pltpu.VMEM((planes * height, chunk), bfloat)] * 3,
        ),
        out_shape=[
            jax.ShapeDtypeStruct((local, own_cols, units), single),
            jax.ShapeDtypeStruct((local, own_cols, units), single),
            jax.ShapeDtypeStruct((local, units, own_cols), single),
        ],
        input_output_aliases=aliases,
        compiler_params=pltpu.CompilerParams(
            dimension_semantics=("arbitrary",) * 3, vmem_limit_bytes=vmem
        ),
        cost_estimate=pl.CostEstimate(
            flops=8 * local * planes * height * model * units,
            bytes_accessed=64 << 20,
            transcendentals=planes * height * units,
        ),
        name="routed_others",
    )(ids, *args)


def masked_scores(scale, q, k, place_q, place_k, piece_q, piece_k):
    allowed = (place_k <= place_q) | ((piece_q == piece_k) & (piece_q > 0))
    return jnp.where(allowed, dot32(q, k, ((1,), (1,))) * scale, -1e30)


def attend_kernel(scale, q_ref, k_ref, v_ref, pq_ref, pk_ref, cq_ref, ck_ref, out_ref, mass_ref):
    scores = masked_scores(
        scale, q_ref[...], k_ref[...], pq_ref[...], pk_ref[...], cq_ref[...], ck_ref[...]
    )
    highest = jnp.max(scores, axis=-1, keepdims=True)
    exponent = jnp.exp(scores - highest)
    total = jnp.sum(exponent, axis=-1, keepdims=True)
    probs = (exponent / total).astype(bfloat)
    out_ref[...] = dot32(probs, v_ref[...], ((1,), (0,))).astype(bfloat)
    mass_ref[0] = highest + jnp.log(total)


def attend_back_kernel(
    scale, q_ref, k_ref, v_ref, da_ref, mass_ref, pq_ref, pk_ref, cq_ref, ck_ref, dq_ref, dk_ref, dv_ref
):
    q, k, v, da = q_ref[...], k_ref[...], v_ref[...], da_ref[...]
    scores = masked_scores(scale, q, k, pq_ref[...], pk_ref[...], cq_ref[...], ck_ref[...])
    probs = jnp.exp(scores - mass_ref[0])
    dprob = dot32(da, v, ((1,), (1,)))
    dsum = jnp.sum(probs * dprob, axis=-1, keepdims=True)
    dscores = (probs * (dprob - dsum)).astype(bfloat)
    dq_ref[...] = dot32(dscores, k, ((1,), (0,))) * scale
    dk = dot32(dscores, q, ((0,), (0,))) * scale
    dv = dot32(probs.astype(bfloat), da, ((0,), (0,)))

    @pl.when(pl.program_id(1) == 0)
    def _():
        dk_ref[...] = dk
        dv_ref[...] = dv

    @pl.when(pl.program_id(1) > 0)
    def _():
        dk_ref[...] += dk
        dv_ref[...] += dv


def attention_call(kernel, name, arrays, masses, marks, out_kinds, products):
    length, width = arrays[0][1].shape
    heads = width // HEAD
    span = min(256, length)
    by_query = pl.BlockSpec((span, HEAD), lambda h, i: (i, h))
    by_head = pl.BlockSpec((length, HEAD), lambda h, i: (0, h))
    mass = pl.BlockSpec((1, span, 1), lambda h, i: (h, i, 0))
    column = pl.BlockSpec((span, 1), lambda h, i: (i, 0))
    row = pl.BlockSpec((1, length), lambda h, i: (0, 0))
    specs = {"query": by_query, "head": by_head, "mass": mass}
    shapes = {"query": (length, width), "head": (length, width), "mass": (heads, length, 1)}
    mark_args = []
    for mark in marks:
        mark_args += [mark[:, None], mark[None, :]]
    return pl.pallas_call(
        kernel,
        grid=(heads, length // span),
        in_specs=[specs[kind] for kind, _ in arrays]
        + [mass] * len(masses)
        + [column, row] * len(marks),
        out_specs=[specs[kind] for kind, _ in out_kinds],
        out_shape=[jax.ShapeDtypeStruct(shapes[kind], dtype) for kind, dtype in out_kinds],
        compiler_params=pltpu.CompilerParams(
            dimension_semantics=("arbitrary",) * 2, vmem_limit_bytes=32 * 1024 * 1024
        ),
        cost_estimate=pl.CostEstimate(
            flops=2 * products * heads * length * length * HEAD,
            bytes_accessed=8 * length * width,
            transcendentals=heads * length * length,
        ),
        name=name,
    )(*[array for _, array in arrays], *masses, *mark_args)


def per_device(
    tokens,
    attn_query,
    attn_key,
    attn_value,
    attn_output,
    norm_in,
    norm_query,
    norm_key,
    norm_mid,
    router,
    expert_gate,
    expert_up,
    expert_down,
    routes,
    pieces,
    cotangent,
):
    n = lax.axis_size("expert")
    m = lax.axis_size("dp")
    rows, model = tokens.shape
    shard = attn_query.shape[0]
    experts = router.shape[1]
    top = routes.shape[1]
    local = expert_gate.shape[0]
    length = rows * n
    near = min(m, 4)
    far = m // near
    half = n // 2
    width = model // n
    heads = width // HEAD
    block = 2 * rows
    mine = lax.axis_index("expert")
    plane = lax.axis_index("dp")
    ready = routes[0, 0] >= 0
    scale = HEAD ** (-0.5)
    order = slot_order()
    slots = jnp.asarray(order, jnp.int32) ^ mine
    cap = -(-2 * min(rows, rows * top // experts + rows // 32) // 16) * 16

    parts = jnp.stack([attn_query, attn_key, attn_value]).reshape(3, shard, n, width)
    parts_out = parts.transpose(2, 0, 1, 3)
    parts = lax.all_to_all(parts_out, "expert", split_axis=0, concat_axis=0, tiled=True)
    parts = parts.transpose(1, 0, 2, 3).reshape(3, n * shard, width)

    def all_rows(part, first=None):
        held, places = gather_steps(part, "dp", m, first)
        out = []
        for kind in range(part.shape[0]):
            full = jnp.zeros((m, n * shard, width), bfloat)
            for at, kd in enumerate(places):
                full = lax.dynamic_update_slice(
                    full, held[at, kind][None], (plane ^ kd, jnp.int32(0), jnp.int32(0))
                )
            out.append(full.reshape(model, width))
        return out

    packed = jnp.concatenate(
        [norm_in[None], norm_query[None], norm_key[None], norm_mid[None], router.T], axis=0
    )
    kinds = packed.shape[0]
    packed = jnp.concatenate(
        [
            jnp.pad(packed.reshape(-1), (0, -kinds * shard % HEAD)).reshape(-1, HEAD),
            routes.T.astype(bfloat).reshape(top * rows // HEAD, HEAD),
            pieces.astype(bfloat).reshape(rows // HEAD, HEAD),
        ],
        axis=0,
    )
    packed = after(packed, parts_out)
    small, places = gather_steps(packed, "dp", m)
    first_rows = swap(after(parts[None], small), "dp", m - 1)
    small = jnp.stack([small[places.index(kd)] for kd in range(m)])
    small = jnp.concatenate(gather_halves(small), axis=0)
    chips = gather_chips(after(jnp.stack([tokens, cotangent]), parts))
    x_even = after(jnp.stack([piece[0] for piece in chips]), first_rows)
    x_odd = swap(x_even, "expert", 1)
    cot_even = jnp.stack([piece[1] for piece in chips])
    cot_odd = swap(cot_even, "expert", 1)
    w_q, w_k, w_v = all_rows(parts, first_rows)
    cut = -(-kinds * shard // HEAD)
    gains = jnp.take(small[:, :, :cut], jnp.asarray([order.index(j) for j in range(n)]), axis=0)
    gains = jnp.take(gains, jnp.arange(n, dtype=jnp.int32) ^ mine, axis=0)
    gains = jnp.take(gains, jnp.arange(m, dtype=jnp.int32) ^ plane, axis=1)
    gains = gains.reshape(n, m, -1)[:, :, : kinds * shard].reshape(n, m, kinds, shard).transpose(2, 1, 0, 3).reshape(kinds, model)
    gain_in, gain_query, gain_key, gain_mid = [gains[i].astype(single) for i in range(4)]
    router_t = gains[4:]
    piece_row = small[:, 0, cut + top * rows // HEAD :].reshape(length)
    route_rows = small[:, :, cut : cut + top * rows // HEAD].reshape(n, m, top, rows)

    x = jnp.concatenate([x_even, x_odd], axis=0).reshape(length, model).astype(single)
    rs_in = lax.rsqrt(jnp.mean(x * x, axis=-1, keepdims=True) + eps_norm)
    normed_b = (x * rs_in * gain_in).astype(bfloat)

    near_groups = [[g * near + i for i in range(near)] for g in range(far)] if far > 1 else None
    cot_planes = lax.all_gather(after(cot_even, w_v), "dp", axis=0, axis_index_groups=near_groups)

    place = (slots[:, None] * rows + jnp.arange(rows, dtype=jnp.int32)[None, :]).reshape(length)
    turn_half = HEAD // 2
    inverse = jnp.exp(jnp.arange(turn_half, dtype=single) * (-2.0 * math.log(rope_base) / HEAD))
    angles = place.astype(single)[:, None] * inverse[None, :]
    cosine = jnp.cos(angles)
    sine = jnp.sin(angles)

    def rotate(values, back):
        out = []
        sn = -sine if back else sine
        for h in range(heads):
            u = values[:, h * HEAD : h * HEAD + turn_half]
            w = values[:, h * HEAD + turn_half : (h + 1) * HEAD]
            out += [u * cosine - w * sn, w * cosine + u * sn]
        return jnp.concatenate(out, axis=-1)

    own_gain_q = lax.dynamic_slice_in_dim(gain_query, mine * width, width)
    own_gain_k = lax.dynamic_slice_in_dim(gain_key, mine * width, width)
    def halves(array):
        return array[: length // 2], array[length // 2 :]

    upper = (
        jnp.arange(block, dtype=jnp.int32)[:, None] <= jnp.arange(block, dtype=jnp.int32)[None, :]
    ).astype(bfloat)
    ids = (mine * local + jnp.arange(local, dtype=jnp.int32)).astype(bfloat)

    def ranks(kd):
        named = route_rows[:, kd]
        hit = jnp.any(named[None] == ids[:, None, None, None], axis=2)
        hit = jnp.concatenate([hit[:, :half], hit[:, half:]], axis=-1)
        rank = lax.dot_general(
            hit.astype(bfloat), upper, (((2,), (0,)), ((), ())), preferred_element_type=single
        )
        return jnp.where(hit, rank, 0.0)

    own_ranks = after(ranks(0)[:, None], cot_odd)

    x_own = tokens.astype(single)

    marks = [place, piece_row.astype(jnp.int32)]

    def forward():
        query_raw = dot32(normed_b, w_q, ((1,), (0,)))
        key_raw = dot32(normed_b, w_k, ((1,), (0,)))
        own_shards = []
        send = attn_output
        for turn in range(m):
            pairs = [(s, ((s % m + turn) % m) * n + s // m) for s in range(m * n)]
            own_shards.append(lax.ppermute(send, ("dp", "expert"), pairs))
        wo = jnp.zeros((m, shard, model), bfloat)
        for turn in range(m):
            wo = lax.dynamic_update_slice(
                wo, own_shards[turn][None], ((plane - turn) % m, jnp.int32(0), jnp.int32(0))
            )
        wo = wo.reshape(width, model)

        squares = jnp.stack([jnp.sum(query_raw**2, axis=-1), jnp.sum(key_raw**2, axis=-1)])
        squares = sum_rows_over_expert(squares.reshape(2, n, rows)).reshape(2, length)
        rs_q = lax.rsqrt(squares[0] / model + eps_norm)[:, None]
        rs_k = lax.rsqrt(squares[1] / model + eps_norm)[:, None]
        value_b = dot32(normed_b, w_v, ((1,), (0,))).astype(bfloat)

        query_b = rotate(query_raw * rs_q * own_gain_q, False).astype(bfloat)
        key_b = rotate(key_raw * rs_k * own_gain_k, False).astype(bfloat)

        attended, masses = attention_call(
            functools.partial(attend_kernel, scale),
            "attend",
            [("query", query_b), ("head", key_b), ("head", value_b)],
            [],
            marks,
            [("query", bfloat), ("mass", single)],
            2,
        )

        projected = [dot32(part, wo, ((1,), (0,))).astype(bfloat) for part in halves(attended)]
        residual = x_own + scatter_sum(*projected)
        rs_mid = lax.rsqrt(jnp.mean(residual * residual, axis=-1, keepdims=True) + eps_norm)
        mid = after(residual * rs_mid * gain_mid, own_ranks).astype(bfloat)
        mid_even, mid_odd = gather_halves(mid)
        kept = (query_raw, key_raw, rs_q, rs_k, query_b, key_b, value_b, wo)
        return kept, masses, attended, residual, rs_mid, mid_even, mid_odd

    kept, masses, attended, residual, rs_mid, mid_even, mid_odd = stage(ready, forward)
    query_raw, key_raw, rs_q, rs_k, query_b, key_b, value_b, wo = kept
    mid_planes = lax.all_gather(after(mid_even, cot_planes), "dp", axis=0, axis_index_groups=near_groups)

    def router_probs_of(mid_rows):
        logits = dot32(router_t, mid_rows.reshape(-1, model), ((1,), (1,)))
        exponent = jnp.exp(logits - jnp.max(logits, axis=0, keepdims=True))
        return exponent / jnp.sum(exponent, axis=0, keepdims=True)

    def local_probs(array):
        return lax.dynamic_slice_in_dim(array, mine * local, local, 0)

    def grouped(even, odd):
        return jnp.concatenate(
            [even.reshape(-1, half, rows), odd.reshape(-1, half, rows)], axis=-1
        )

    router_probs = grouped(router_probs_of(mid_even), router_probs_of(mid_odd))
    fixed_ids = jnp.stack([plane % near, mine * local])

    def by_group(blocks):
        return jnp.stack([blocks[:half], blocks[half:]], axis=1).reshape(n)

    def backward():
        own_out = routed_own(
            fixed_ids,
            cap,
            near,
            far,
            own_ranks,
            local_probs(router_probs)[:, None],
            [mid_even[None], mid_odd[None]],
            [cot_even[None], cot_odd[None]],
            expert_gate,
            expert_up,
            expert_down,
            router_probs.transpose(1, 0, 2),
            router_t,
        )
        hidden_own, gate_lin_own, up_lin_own, x_own_cut, d_own_cut = own_out[:5]
        moe_even, moe_odd, dmid_even, dmid_odd, dlogits = own_out[5:]
        dmid = scatter_sum(dmid_even, dmid_odd)
        scaled = dmid * gain_mid
        mid_grad = jnp.sum(dmid * (residual * rs_mid), axis=0)
        inner = jnp.mean(scaled * residual, axis=-1, keepdims=True)
        dres = cotangent.astype(single) + rs_mid * (scaled - residual * (rs_mid * rs_mid * inner))
        dres_chips = gather_chips(dres.astype(bfloat))
        dres_even = jnp.stack(dres_chips)
        dres_odd = swap(dres_even, "expert", 1).reshape(-1, model)
        dres_even = dres_even.reshape(-1, model)
        datt_b = jnp.concatenate(
            [dot32(part, wo, ((1,), (1,))) for part in (dres_even, dres_odd)], axis=0
        )
        datt_b = datt_b.astype(bfloat)

        moe_pairs = jnp.stack(pair_sums(moe_even, moe_odd))
        cot_planes_odd = swap(cot_planes, "expert", 1)
        gate_tables = [swap(local_probs(router_probs), "dp", kd) for kd in range(1, near)]

        dq_rot, dk_rot, dv = attention_call(
            functools.partial(attend_back_kernel, scale),
            "attend_back",
            [("query", query_b), ("head", key_b), ("head", value_b), ("query", datt_b)],
            [masses],
            marks,
            [("query", single), ("head", single), ("head", single)],
            5,
        )
        dq_un = rotate(dq_rot, True)
        dk_un = rotate(dk_rot, True)
        inners = jnp.stack(
            [
                jnp.sum(dq_un * own_gain_q * query_raw, axis=-1),
                jnp.sum(dk_un * own_gain_k * key_raw, axis=-1),
            ]
        )
        inners = sum_rows_over_expert(inners.reshape(2, n, rows)).reshape(2, length)
        query_gain_grad = jnp.sum(dq_un * query_raw * rs_q, axis=0)
        key_gain_grad = jnp.sum(dk_un * key_raw * rs_k, axis=0)
        dq_b = (
            rs_q * dq_un * own_gain_q - query_raw * (rs_q**3 / model * inners[0][:, None])
        ).astype(bfloat)
        dk_b = (
            rs_k * dk_un * own_gain_k - key_raw * (rs_k**3 / model * inners[1][:, None])
        ).astype(bfloat)
        dv_b = dv.astype(bfloat)
        dnormed_part = [
                (
                    dot32(dq_part, w_q, ((1,), (1,)))
                    + dot32(dk_part, w_k, ((1,), (1,)))
                    + dot32(dv_part, w_v, ((1,), (1,)))
                ).astype(bfloat)
                for dq_part, dk_part, dv_part in zip(halves(dq_b), halves(dk_b), halves(dv_b))
        ]
        output_part = dot32(dres_even, attended[: length // 2], ((0,), (0,))) + dot32(
            dres_odd, attended[length // 2 :], ((0,), (0,))
        )
        early = jnp.stack([dot32(normed_b, dv_b, ((0,), (0,))), output_part]).astype(bfloat)
        late = jnp.stack([dot32(normed_b, part, ((0,), (0,))) for part in (dq_b, dk_b)])
        late = late.astype(bfloat)
        return (
            own_out,
            dres,
            dres_even,
            dres_odd,
            mid_grad,
            query_gain_grad,
            key_gain_grad,
            dq_b,
            dk_b,
            dv_b,
            dnormed_part,
            moe_pairs,
            cot_planes_odd,
            gate_tables,
            early,
            late,
        )

    (
        own_out,
        dres,
        dres_even,
        dres_odd,
        mid_grad,
        query_gain_grad,
        key_gain_grad,
        dq_b,
        dk_b,
        dv_b,
        dnormed_part,
        moe_pairs,
        cot_planes_odd,
        gate_tables,
        early,
        late,
    ) = stage(ready, backward)
    hidden_own, gate_lin_own, up_lin_own, x_own_cut, d_own_cut = own_out[:5]
    moe_even, moe_odd, dmid_even, dmid_odd, dlogits = own_out[5:]
    dnormed = scatter_sum(*dnormed_part)
    dnormed_part = dnormed_part[0]

    dlogits = dlogits.transpose(1, 0, 2).astype(bfloat)
    router_grad = dot32(
        dlogits[:, :, :rows].reshape(experts, -1), mid_even.reshape(-1, model), ((1,), (0,))
    ) + dot32(dlogits[:, :, rows:].reshape(experts, -1), mid_odd.reshape(-1, model), ((1,), (0,)))

    mid_planes = [mid_planes, swap(mid_planes, "expert", 1)]
    cot_planes = [cot_planes, cot_planes_odd]
    def add_sequences(masks, more, *earlier):
        planes = [plane % near ^ kd for kd in masks]
        return routed_others(
            jnp.concatenate([plane[None] % near, jnp.full((1,), len(masks), jnp.int32), jnp.stack(planes)]),
            cap,
            near,
            far,
            after(jnp.stack([ranks(kd) for kd in masks], axis=1), *earlier),
            jnp.stack([gate_tables[kd - 1] for kd in masks], axis=1),
            mid_planes,
            cot_planes,
            expert_gate,
            expert_up,
            expert_down,
            more,
        )

    late = lax.psum_scatter(late, "dp", scatter_dimension=1, tiled=True)
    early = lax.psum_scatter(early, "dp", scatter_dimension=1, tiled=True)
    cut = half // 2
    moe_arrived = swap(moe_pairs[cut:], "expert", 2 * cut)
    weight_sums = add_sequences(list(range(1, near - 1)), None, dnormed_part)
    dnormed = after(dnormed, weight_sums[0])
    moe_sums = moe_pairs[:cut].astype(single) + after(moe_arrived, weight_sums[0]).astype(single)
    while moe_sums.shape[0] > 1:
        cut = moe_sums.shape[0] // 2
        arrived = swap(moe_sums[cut:].astype(bfloat), "expert", 2 * cut)
        moe_sums = moe_sums[:cut] + arrived.astype(single)
    output = (residual + moe_sums[0]).astype(bfloat)
    summed = jnp.concatenate([early[:1], late], axis=0)
    moved = lax.all_to_all(
        after(summed, weight_sums[0]).reshape(3, n, shard, width).transpose(1, 0, 2, 3),
        "expert",
        split_axis=0,
        concat_axis=0,
        tiled=True,
    )
    moved = moved.transpose(1, 2, 0, 3).reshape(3, shard, model).astype(single)
    value_grad, query_grad, key_grad = moved[0], moved[1], moved[2]
    output_sum = after(early[1], weight_sums[0]).reshape(model // m, m, shard).transpose(1, 2, 0)
    pieces_here = []
    for turn in range(m):
        pairs = [(((s % m + turn) % m) * n + s // m, s) for s in range(m * n)]
        sent = lax.dynamic_index_in_dim(output_sum, (plane - turn) % m, 0, keepdims=False)
        pieces_here.append(lax.ppermute(sent, ("dp", "expert"), pairs))
    shard_at = (plane * n + mine) % m
    output_grad = jnp.take(
        jnp.stack(pieces_here), (jnp.arange(m, dtype=jnp.int32) - shard_at) % m, axis=0
    )
    output_grad = output_grad.transpose(1, 0, 2).reshape(shard, model).astype(single)

    rs_own = rs_in[:rows]
    scaled_in = dnormed * gain_in
    inner_in = jnp.mean(scaled_in * x_own, axis=-1, keepdims=True)
    input_grad = dres + rs_own * (scaled_in - x_own * (rs_own * rs_own * inner_in))
    in_grad = jnp.sum(dnormed * x_own * rs_own, axis=0)

    def placed(part):
        return lax.dynamic_update_slice(jnp.zeros((model,), single), part, (mine * width,))

    small_grad = jnp.concatenate(
        [
            in_grad[None],
            placed(query_gain_grad)[None],
            placed(key_gain_grad)[None],
            mid_grad[None],
            router_grad,
        ],
        axis=0,
    ).reshape(kinds, m, n, shard)
    small_grad = jnp.take(small_grad, jnp.arange(n, dtype=jnp.int32) ^ mine, axis=2)
    small_pair = small_grad[:, :, 0::2] + swap(small_grad[:, :, 1::2], "expert", 1)
    small_sum = small_pair[:, :, 0]
    for k in range(2, n, 2):
        small_sum = small_sum + swap(small_pair[:, :, k // 2], "expert", k)
    small_sum = jnp.take(small_sum, jnp.arange(m, dtype=jnp.int32) ^ plane, axis=1)
    total = small_sum[:, 0]
    for k in range(1, m):
        total = total + swap(small_sum[:, k], "dp", k)

    own_rows = [x_own_cut, d_own_cut, hidden_own, gate_lin_own, up_lin_own]
    weight_sums = add_sequences([near - 1], own_rows + list(weight_sums))
    gate_grad, up_grad, down_grad = weight_sums
    span = model // m

    def sum_over_far(parts):
        if far == 1:
            return parts[0]
        parts = jnp.take(parts, jnp.arange(far, dtype=jnp.int32) ^ (plane // near), axis=0)
        total = parts[0]
        for k in range(1, far):
            total = total + swap(parts[k].astype(bfloat), "dp", k * near).astype(single)
        return total

    units = expert_gate.shape[2]
    gate_grad, up_grad = [
        sum_over_far(grad.reshape(local, far, span, units).transpose(1, 0, 2, 3))
        for grad in (gate_grad, up_grad)
    ]
    down_grad = sum_over_far(down_grad.reshape(local, units, far, span).transpose(2, 0, 1, 3))

    return (
        output,
        input_grad,
        query_grad,
        key_grad,
        value_grad,
        output_grad,
        total[0],
        total[1],
        total[2],
        total[3],
        total[4:].T,
        gate_grad,
        up_grad,
        down_grad,
    )


def solution(mesh):
    both = ("dp", "expert")
    in_specs = (
        [P(both, None)] * 5
        + [P(both)] * 4
        + [P(both, None)]
        + [P("expert", None, None)] * 3
        + [P(both, None), P(both), P(both, None)]
    )
    out_specs = (
        [P(both, None)] * 6
        + [P(both)] * 4
        + [P(both, None)]
        + [P("expert", "dp", None)] * 2
        + [P("expert", None, "dp")]
    )
    return jax.shard_map(
        per_device,
        mesh=mesh,
        in_specs=tuple(in_specs),
        out_specs=tuple(out_specs),
        check_vma=False,
    )
```
